256 devices in a mesh: blk: 64 (over x, z, core), rep: 4 (over y).
Axes of the slice: x: 4, y: 4, z: 8, core: 2. Of those that a mesh axis runs over, the one named last changes fastest.
Arguments:
- right_side: float32 [64, 262144], P(None, 'blk'), may hold values from -6 to 6
- points: float32 [3, 262144], P(None, 'blk'), may hold values from -1 to 544, as said below
- active: int32 [64, 5], replicated, may hold values 0 or 1
Outputs:
- posterior_mean: float32 [64, 262144], P(None, 'blk')
- residual: float32 [64, 262144], P(None, 'blk')
The draws below stay inside these ranges and needn't reach their ends.
Inputs may be any that keep to these rules, and one draw needn't show every extreme that they name: `points`: point coordinates in lattice units.
All inputs are finite; a program needn't handle non-finite values.
Results may differ from the reference program's by a relative error of at most 0.0003.
Values sent between devices are 32-bit elements; how exact they have to be, the bound alone decides.
No kernel may reach another device: no remote copies, remote signals or barrier semaphores. Data moves between devices by JAX's collectives and lax.ppermute only.
A program may use at most 128 MiB of HBM per device.

```python
import jax
import jax.numpy as jnp
from jax import lax

BX = 8
BY = 16
BZ = 16
R = 64
ITERS = 2
B = 2048
NB = 128
N = 262144
N_BLK = 64


def draw_points(key, part):
    local = jnp.arange(B, dtype=jnp.int32)
    plane = local // (BY * BZ)
    across = local // BZ % BY
    depth = local % BZ
    block = jnp.arange(NB, dtype=jnp.int32)
    block_keys = jax.random.split(jax.random.fold_in(key, 11), NB)
    order = jax.vmap(lambda single: jax.random.permutation(single, B))(block_keys).astype(jnp.int32)
    strip = (block // 2)[:, None]
    side = (block % 2)[:, None]
    coord_x = (BX * strip + plane[order]).astype(jnp.float32)
    coord_y = (BY * side + across[order]).astype(jnp.float32)
    coord_z = (depth[order] + 0 * strip).astype(jnp.float32)
    lattice = jnp.stack([coord_x, coord_y, coord_z]).reshape(3, N)
    jitter_key = jax.random.fold_in(key, 12)
    jitter = jax.random.uniform(jitter_key, (3, N), jnp.float32, -0.1, 0.1)
    return lattice + jitter


def place_ends(values, key, smallest, high):
    longest = values.shape.index(max(values.shape))
    spots = []
    for shift in (0, 1):
        where = [jax.random.randint(jax.random.fold_in(key, axis), (), 0, length) for axis, length in enumerate(values.shape)]
        where[longest] = (where[longest] + shift) % values.shape[longest]
        spots.append(tuple(where))
    return values.at[spots[0]].set(smallest).at[spots[1]].set(high)


def block_scale(key, shape, cuts, smallest, top_value):
    def one(dim, shards_of):
        heights = jax.random.uniform(jax.random.fold_in(jax.random.fold_in(key, 6), dim), (shards_of,), jnp.float32, smallest / len(cuts), top_value / len(cuts))
        return jnp.repeat(jnp.exp(heights), shape[dim] // shards_of).reshape((-1,) + (1,) * (len(shape) - dim - 1))

    loudness = one(*cuts[0])
    for cut in cuts[1:]:
        loudness = loudness * one(*cut)
    return loudness


def centred(own_key, shape, spread, reach, cuts=(), held_as=jnp.bfloat16):
    level = block_scale(own_key, shape, cuts, -0.22, 0.18) if cuts else 1.0
    values = jax.random.normal(own_key, shape, jnp.float32) * spread * level
    return jnp.minimum(jnp.maximum(values, -reach), reach).astype(held_as)


def setup_inputs(seed: int = 0) -> dict:
    seeds = jax.random.split(jax.random.key(seed), 4)
    return {
        "right_side": centred(seeds[0], (R, N), 1.0, 6.0, ((1, 64),), jnp.float32),
        "points": draw_points(jax.random.fold_in(seeds[3], 71), 0),
        "active": place_ends((jax.random.randint(seeds[2], (N_BLK, 5), 0, 4) < 3).astype(jnp.int32), jax.random.fold_in(seeds[2], 1), 0, 1),
    }


support_radius = 2.5
noise_level = 8.0

def wendland(rows, cols):
    delta_x = rows[0][:, None] - cols[0][None, :]
    delta_y = rows[1][:, None] - cols[1][None, :]
    delta_z = rows[2][:, None] - cols[2][None, :]
    scaled = jnp.sqrt(delta_x * delta_x + delta_y * delta_y + delta_z * delta_z) / support_radius
    inside = jnp.maximum(1.0 - scaled, 0.0)
    square = inside * inside
    return square * square * (4.0 * scaled + 1.0)

def apply_rows(vector, kernel_tile):
    return lax.dot_general(vector, kernel_tile, (((1,), (1,)), ((), ())), precision=lax.Precision.HIGHEST, preferred_element_type=jnp.float32)

def pair_flags(active, column, count):
    here = lax.dynamic_slice_in_dim(active, column, 1, 0)[0].astype(jnp.float32)
    before = lax.dynamic_slice_in_dim(active, jnp.maximum(column - 1, 0).astype(jnp.int32), 1, 0)[0].astype(jnp.float32)
    has_before = (column >= 1).astype(jnp.float32)
    has_after = (column + 1 < count).astype(jnp.float32)
    table = []
    for c in range(2):
        entry = []
        for k in range(6):
            if k < 2:
                entry.append(before[1 + 2 * k + c] * has_before)
            elif k == 2 + c:
                entry.append(has_after * 0.0 + 1.0)
            elif k < 4:
                entry.append(here[0])
            else:
                entry.append(here[1 + 2 * c + (k - 4)] * has_after)
        table.append(entry)
    return table

def operator(vector, points, active):
    count = active.shape[0]
    padded_pts = jnp.pad(points.reshape(3, count, 2 * B), ((0, 0), (1, 1), (0, 0)))
    padded_vec = jnp.pad(vector.reshape(R, count, 2 * B), ((0, 0), (1, 1), (0, 0)))

    def column_image(column):
        window_pts = lax.dynamic_slice_in_dim(padded_pts, column, 3, 1).reshape(3, 6 * B)
        window_vec = lax.dynamic_slice_in_dim(padded_vec, column, 3, 1).reshape(R, 6 * B)
        flags = pair_flags(active, column, count)
        pieces = []
        for c in range(2):
            rows = window_pts[:, (2 + c) * B:(3 + c) * B]
            total = jnp.zeros((R, B), jnp.float32)
            for k in range(6):
                kernel_tile = wendland(rows, window_pts[:, k * B:(k + 1) * B])
                total = total + flags[c][k] * apply_rows(window_vec[:, k * B:(k + 1) * B], kernel_tile)
            pieces.append(total)
        return jnp.concatenate(pieces, axis=1)
    images = lax.map(column_image, jnp.arange(count, dtype=jnp.int32))
    return jnp.transpose(images, (1, 0, 2)).reshape(R, count * 2 * B) + noise_level * vector

def reference(right_side, points, active):
    solution = jnp.zeros_like(right_side)
    residual = right_side
    direction = right_side
    norm_now = lax.optimization_barrier(jnp.sum(residual * residual, axis=1))
    for step in range(ITERS):
        image = operator(direction, points, active)
        alpha = norm_now / lax.optimization_barrier(jnp.sum(direction * image, axis=1))
        solution = solution + alpha[:, None] * direction
        residual = residual - alpha[:, None] * image
        norm_next = lax.optimization_barrier(jnp.sum(residual * residual, axis=1))
        direction = residual + (norm_next / norm_now)[:, None] * direction
        norm_now = norm_next
    return (right_side - noise_level * solution, residual)
```

```python
from functools import partial

import jax
import jax.numpy as jnp
from jax import lax
from jax.sharding import PartitionSpec as P

B = 2048


support_radius = 2.5
noise_level = 8.0


def from_behind(block, axis, distance):
    devices = range(lax.axis_size(axis))
    route = [(i - distance, i) for i in devices if i - distance in devices]
    return lax.ppermute(block, axis, route)


def wendland(rows, cols):
    delta_x = rows[0][:, None] - cols[0][None, :]
    delta_y = rows[1][:, None] - cols[1][None, :]
    delta_z = rows[2][:, None] - cols[2][None, :]
    scaled = jnp.sqrt(delta_x * delta_x + delta_y * delta_y + delta_z * delta_z) / support_radius
    inside = jnp.maximum(1.0 - scaled, 0.0)
    square = inside * inside
    return square * square * (4.0 * scaled + 1.0)


def apply_rows(vector, kernel_tile):
    return lax.dot_general(
        vector,
        kernel_tile,
        (((1,), (1,)), ((), ())),
        precision=lax.Precision.HIGHEST,
        preferred_element_type=jnp.float32,
    )


def apply_cols(vector, kernel_tile):
    return jnp.dot(
        vector, kernel_tile, precision=lax.Precision.HIGHEST, preferred_element_type=jnp.float32
    )


def pair_flags(active, column, count):
    here = lax.dynamic_slice_in_dim(active, column, 1, 0)[0].astype(jnp.float32)
    before = lax.dynamic_slice_in_dim(active, jnp.maximum(column - 1, 0), 1, 0)[0].astype(
        jnp.float32
    )
    has_before = (column >= 1).astype(jnp.float32)
    has_after = (column + 1 < count).astype(jnp.float32)
    table = []
    for c in range(2):
        entry = []
        for k in range(6):
            if k < 2:
                entry.append(before[1 + 2 * k + c] * has_before)
            elif k == 2 + c:
                entry.append(has_after * 0.0 + 1.0)
            elif k < 4:
                entry.append(here[0])
            else:
                entry.append(here[1 + 2 * c + (k - 4)] * has_after)
        table.append(entry)
    return table


def gated(flag, compute, operands):
    return flag * compute(*operands)


def place_rows(values, start, total):
    return lax.dynamic_update_slice_in_dim(
        jnp.zeros((values.shape[0], total), jnp.float32), values, start, 1
    )


def exchange(values, mask, axis):
    devices = range(lax.axis_size(axis))
    return lax.ppermute(values, axis, [(i, i ^ mask) for i in devices])


def sum_over_blk(values):
    for base in (1, 4, 16):
        near = values + exchange(values, base, "blk")
        far = exchange(values, 2 * base, "blk") + exchange(values, 3 * base, "blk")
        values = near + far
    return values


def sum_over_rep(values):
    member = lax.axis_index("rep")
    width = values.shape[1] // 4

    def part(index):
        return lax.dynamic_slice_in_dim(values, index * width, width, 1)

    mine = part(member) + exchange(part(member ^ 1), 1, "rep")
    mine = mine + (exchange(part(member ^ 2), 2, "rep") + exchange(part(member ^ 3), 3, "rep"))
    total = jnp.zeros_like(values)
    for mask in range(4):
        piece = mine if mask == 0 else exchange(mine, mask, "rep")
        total = lax.dynamic_update_slice_in_dim(total, piece, (member ^ mask) * width, 1)
    return total


def shards(right_side, points, active):
    count = lax.axis_size("blk")
    column = lax.axis_index("blk")
    groups = lax.axis_size("rep")
    member = lax.axis_index("rep")
    flags = pair_flags(active, column, count)
    rows_each = B // groups
    row_start = member * rows_each
    sides = right_side.shape[0]

    def row_slice(array, c):
        return lax.dynamic_slice_in_dim(array, c * B + row_start, rows_each, 1)

    def fetch(stored, index):
        return stored[index]

    pts_next = from_behind(points, "blk", -1)
    makers = [
        partial(wendland, row_slice(points, c), points[:, c * B : (c + 1) * B]) for c in range(2)
    ]
    makers.append(partial(wendland, row_slice(points, 0), points[:, B : 2 * B]))
    for c in range(2):
        for k in range(2):
            makers.append(partial(wendland, row_slice(points, c), pts_next[:, k * B : (k + 1) * B]))
    stored = [maker() for maker in makers]

    def matvec(vector):
        vec_next = from_behind(vector, "blk", -1)
        own_rows = [row_slice(vector, c) for c in range(2)]
        row_terms = [apply_rows(vector[:, c * B : (c + 1) * B], fetch(stored, c)) for c in range(2)]
        across_tile = fetch(stored, 2)
        row_terms[0] = row_terms[0] + gated(
            flags[0][3], apply_rows, (vector[:, B : 2 * B], across_tile)
        )
        across_back = gated(flags[0][3], apply_cols, (own_rows[0], across_tile))
        next_terms = [jnp.zeros((sides, B), jnp.float32), jnp.zeros((sides, B), jnp.float32)]
        for c in range(2):
            for k in range(2):
                kernel_tile = fetch(stored, 3 + 2 * c + k)
                flag = flags[c][4 + k]
                row_terms[c] = row_terms[c] + gated(
                    flag, apply_rows, (vec_next[:, k * B : (k + 1) * B], kernel_tile)
                )
                next_terms[k] = next_terms[k] + gated(flag, apply_cols, (own_rows[c], kernel_tile))
        own_full = jnp.concatenate(
            [
                place_rows(row_terms[0], row_start, B),
                across_back + place_rows(row_terms[1], row_start, B),
            ],
            axis=1,
        )
        returned = from_behind(jnp.concatenate(next_terms, axis=1), "blk", 1)
        return sum_over_rep(own_full + returned)

    r0 = right_side
    u0 = matvec(r0)
    first = sum_over_blk(jnp.stack([jnp.sum(r0 * r0, axis=1), jnp.sum(r0 * u0, axis=1)]))
    u1 = matvec(u0)
    s00, s01 = first[0], first[1]
    image_norm = noise_level * s00 + s01
    alpha = (s00 / image_norm)[:, None]
    keep = (s01 / image_norm)[:, None]
    r1 = keep * r0 - alpha * u0
    k_r1 = keep * u0 - alpha * u1
    image0 = noise_level * r0 + u0
    second = sum_over_blk(
        jnp.stack(
            [jnp.sum(r1 * r1, axis=1), jnp.sum(r1 * k_r1, axis=1), jnp.sum(r1 * image0, axis=1)]
        )
    )
    rr1 = second[0]
    beta = rr1 / s00
    norm1 = noise_level * rr1 + second[1] + 2.0 * beta * second[2] + beta * beta * image_norm
    alpha1 = (rr1 / norm1)[:, None]
    beta = beta[:, None]
    direction = r1 + beta * r0
    image = noise_level * direction + k_r1 + beta * u0
    residual = r1 - alpha1 * image
    posterior = r0 - noise_level * (alpha * r0 + alpha1 * direction)
    return (posterior, residual)


def solution(mesh):
    return jax.shard_map(
        shards,
        mesh=mesh,
        in_specs=(P(None, "blk"), P(None, "blk"), P()),
        out_specs=(P(None, "blk"), P(None, "blk")),
        check_vma=False,
    )
```

```python
from functools import partial

import jax
import jax.numpy as jnp
from jax import lax
from jax.experimental import pallas as pl
from jax.experimental.pallas import tpu as pltpu
from jax.sharding import PartitionSpec as P

B = 2048
SUB = 64
TILE = 128
STRIP = 256
BATCH = 4
CELLS_X = 4
CELLS_Y = 8
CELLS = CELLS_X * CELLS_Y
FAR = 1.0e6

support_radius = 2.5
noise_level = 8.0
shift = noise_level + 1.0
profile_scale = 4.0 / support_radius**5
VMEM = pl.BlockSpec(memory_space=pltpu.VMEM)
SMEM = pl.BlockSpec(memory_space=pltpu.SMEM)
PARAMS = pltpu.CompilerParams(vmem_limit_bytes=48 * 1024 * 1024)


def from_behind(block, axis, distance):
    devices = range(lax.axis_size(axis))
    route = [(i - distance, i) for i in devices if i - distance in devices]
    return lax.ppermute(block, axis, route)


def exchange(values, mask, axis):
    devices = range(lax.axis_size(axis))
    return lax.ppermute(values, axis, [(i, i ^ mask) for i in devices])


def sum_over_blk(values):
    for base in (1, 4, 16):
        near = values + exchange(values, base, "blk")
        far = exchange(values, 2 * base, "blk") + exchange(values, 3 * base, "blk")
        values = near + far
    return values


def split3(values):
    high = values.astype(jnp.bfloat16)
    rest = values - high.astype(jnp.float32)
    middle = rest.astype(jnp.bfloat16)
    low = (rest - middle.astype(jnp.float32)).astype(jnp.bfloat16)
    return high, middle, low


def one_hot_strip(rank, start):
    place = lax.broadcasted_iota(jnp.int32, (STRIP, B), 0) + start
    return jnp.where(rank == place, 1.0, 0.0).astype(jnp.bfloat16)


def cell_of(values, cells):
    low = jnp.min(values, axis=1, keepdims=True)
    high = jnp.max(values, axis=1, keepdims=True)
    scaled = (values - low) * (cells / jnp.maximum(high - low, 1e-30))
    return jnp.minimum(jnp.floor(scaled), cells - 1.0)


def sort_kernel(points_ref, vector_ref, rows_ref, cols_ref, rank_ref, feature_ref, split_ref):
    upper = lax.broadcasted_iota(jnp.int32, (TILE, TILE), 0) <= lax.broadcasted_iota(
        jnp.int32, (TILE, TILE), 1
    )
    upper = jnp.where(upper, 1.0, 0.0).astype(jnp.bfloat16)
    lower = lax.broadcasted_iota(jnp.int32, (CELLS, CELLS), 0) > lax.broadcasted_iota(
        jnp.int32, (CELLS, CELLS), 1
    )
    lower = jnp.where(lower, 1.0, 0.0)
    number = lax.broadcasted_iota(jnp.int32, (CELLS, TILE), 0).astype(jnp.float32)
    feature_ref[16:32, :] = jnp.zeros((16, B), jnp.float32)
    split_ref[96:128, :] = jnp.zeros((32, B), jnp.bfloat16)
    for c in range(2):
        span = slice(c * B, (c + 1) * B)
        cell = cell_of(points_ref[0:1, span], CELLS_X) * CELLS_Y + cell_of(
            points_ref[1:2, span], CELLS_Y
        )
        base = jnp.zeros((CELLS, TILE), jnp.float32)
        chosen, place = [], []
        for t in range(B // TILE):
            hit = jnp.where(number == cell[:, t * TILE : (t + 1) * TILE], 1.0, 0.0)
            count = jnp.dot(hit.astype(jnp.bfloat16), upper, preferred_element_type=jnp.float32)
            chosen.append(hit)
            place.append(count + base)
            base = base + count[:, TILE - 1 :]
        offset = jnp.dot(
            lower, base, precision=lax.Precision.HIGHEST, preferred_element_type=jnp.float32
        )
        for t in range(B // TILE):
            rank = jnp.sum(chosen[t] * (place[t] + (offset - 1.0)), axis=0, keepdims=True)
            rank_ref[0:1, c * B + t * TILE : c * B + (t + 1) * TILE] = rank.astype(jnp.int32)
        feature_ref[0:16, :] = vector_ref[:, span]
        feature_ref[16:19, :] = points_ref[:, span]
        for k, part in enumerate(split3(feature_ref[...])):
            split_ref[32 * k : 32 * k + 32, :] = part
        rank = rank_ref[0:1, span]
        for k in range(B // STRIP):
            found = lax.dot_general(
                one_hot_strip(rank, k * STRIP),
                split_ref[...],
                (((1,), (1,)), ((), ())),
                preferred_element_type=jnp.float32,
            )
            found = found + pltpu.roll(found, 96, 1) + pltpu.roll(found, 64, 1)
            spot = slice(c * B + k * STRIP, c * B + (k + 1) * STRIP)
            cols_ref[spot, :] = found
            rows_ref[:, spot] = found.T[0:24, :]


def sort_points(points, vector):
    width = 2 * B
    return pl.pallas_call(
        sort_kernel,
        out_shape=(
            jax.ShapeDtypeStruct((24, width), jnp.float32),
            jax.ShapeDtypeStruct((width, TILE), jnp.float32),
            jax.ShapeDtypeStruct((8, width), jnp.int32),
        ),
        in_specs=[VMEM, VMEM],
        out_specs=(VMEM, VMEM, VMEM),
        scratch_shapes=[pltpu.VMEM((32, B), jnp.float32), pltpu.VMEM((128, B), jnp.bfloat16)],
        compiler_params=PARAMS,
        name="sort_points",
    )(points, vector)


def unsort_kernel(sorted_ref, rank_ref, out_ref, split_ref, total_ref):
    for c in range(2):
        span = slice(c * B, (c + 1) * B)
        for k, part in enumerate(split3(sorted_ref[:, span])):
            split_ref[16 * k : 16 * k + 16, :] = part
        rank = rank_ref[0:1, span]
        for k in range(B // STRIP):
            found = jnp.dot(
                split_ref[:, k * STRIP : (k + 1) * STRIP],
                one_hot_strip(rank, k * STRIP),
                preferred_element_type=jnp.float32,
            )
            total_ref[...] = found if k == 0 else total_ref[...] + found
        out_ref[:, span] = (total_ref[0:16, :] + total_ref[16:32, :]) + total_ref[32:48, :]


def unsort(values, rank):
    return pl.pallas_call(
        unsort_kernel,
        out_shape=jax.ShapeDtypeStruct(values.shape, jnp.float32),
        in_specs=[VMEM, VMEM],
        out_specs=VMEM,
        scratch_shapes=[pltpu.VMEM((48, B), jnp.bfloat16), pltpu.VMEM((48, B), jnp.float32)],
        compiler_params=PARAMS,
        name="unsort",
    )(values, rank)


def apply_kernel(
    own, tiles, stride, counts_ref, list_ref, cols_ref, coords_ref, vec_ref, *rest
):
    if own:
        add_ref = None
        out_ref, left_xyz, right_xyz, left_w, right_w, target, tile_a, tile_b = rest
    else:
        add_ref, out_ref, left_xyz, right_xyz, left_w, right_w, target, tile_a, tile_b = rest
    lane = lax.broadcasted_iota(jnp.int32, (8, TILE), 1)
    is_left = lane < SUB

    def spread(values):
        turned = pltpu.roll(values, SUB, 1)
        mask = jnp.concatenate([is_left] * (values.shape[0] // 8), axis=0)
        zero = jnp.zeros_like(values)
        return (
            jnp.where(mask, values, zero),
            jnp.where(mask, zero, turned),
            jnp.where(mask, turned, zero),
            jnp.where(mask, zero, values),
        )

    def weights(values):
        high = values.astype(jnp.bfloat16)
        low = (values - high.astype(jnp.float32)).astype(jnp.bfloat16)
        return jnp.concatenate([high, low], axis=0)

    def prepare(t, carry):
        spot = pl.ds(pl.multiple_of(t * TILE, TILE), TILE)
        xyz = spread(coords_ref[:, spot])
        left_xyz[2 * t] = xyz[0]
        right_xyz[2 * t] = xyz[1]
        left_xyz[2 * t + 1] = xyz[2]
        right_xyz[2 * t + 1] = xyz[3]
        vec = spread(vec_ref[:, spot])
        left_w[2 * t] = weights(vec[0])
        right_w[2 * t] = weights(vec[1])
        left_w[2 * t + 1] = weights(vec[2])
        right_w[2 * t + 1] = weights(vec[3])
        return carry

    lax.fori_loop(0, tiles, prepare, 0)
    left_xyz[2 * tiles] = jnp.where(is_left, FAR, 0.0)
    right_xyz[2 * tiles] = jnp.where(is_left, 0.0, FAR)
    left_w[2 * tiles] = jnp.zeros((32, TILE), jnp.bfloat16)
    right_w[2 * tiles] = jnp.zeros((32, TILE), jnp.bfloat16)

    def pair(base, slot, tile):
        first = list_ref[base + 2 * slot]
        second = list_ref[base + 2 * slot + 1]
        xyz = left_xyz[first] + right_xyz[second]
        weight = left_w[first] + right_w[second]
        for r in range(TILE // 16):
            rows = slice(16 * r, 16 * r + 16)
            dx = target[0, rows, :] - xyz[0:1, :]
            dy = target[1, rows, :] - xyz[1:2, :]
            dz = target[2, rows, :] - xyz[2:3, :]
            square = jnp.maximum(dx * dx + dy * dy + dz * dz, 1e-30)
            distance = square * lax.rsqrt(square)
            inside = jnp.maximum(support_radius - distance, 0.0)
            inside = inside * inside
            value = (inside * inside) * (distance + 0.25 * support_radius)
            high = value.astype(jnp.bfloat16)
            tile[rows, 0:TILE] = high
            tile[rows, TILE : 2 * TILE] = (value - high.astype(jnp.float32)).astype(jnp.bfloat16)
        return jnp.concatenate([weight, weight], axis=1)

    def apply(weight, tile):
        return lax.dot_general(
            weight, tile[...], (((1,), (1,)), ((), ())), preferred_element_type=jnp.float32
        )

    def row(j, carry):
        spot = pl.ds(pl.multiple_of(j * TILE, TILE), TILE)
        count = counts_ref[j]
        for axis in range(3):
            target[axis] = jnp.broadcast_to(cols_ref[spot, 16 + axis : 17 + axis], (TILE, TILE))

        def step(n, total):
            base = j * stride + n * BATCH
            weight_a = pair(base, 0, tile_a)
            weight_b = pair(base, 1, tile_b)
            return total + (apply(weight_a, tile_a) + apply(weight_b, tile_b))

        total = lax.fori_loop(
            0, (count + BATCH - 1) // BATCH, step, jnp.zeros((32, TILE), jnp.float32)
        )
        image = (total[0:16, :] + total[16:32, :]) * profile_scale
        if own:
            held = (left_w[2 * j] + right_w[2 * j + 1]).astype(jnp.float32)
            out_ref[:, spot] = image - (held[0:16, :] + held[16:32, :])
        else:
            out_ref[:, spot] = image + add_ref[:, spot]
        return carry

    lax.fori_loop(0, out_ref.shape[1] // TILE, row, 0)


def apply_pairs(lists, cols, coords, vector, added=None):
    counts, table = lists
    own = added is None
    tiles = vector.shape[1] // TILE
    operands = [counts, table.reshape(-1), cols, coords, vector] + ([] if own else [added])
    slots = 2 * tiles + 1
    return pl.pallas_call(
        partial(apply_kernel, own, tiles, table.shape[1]),
        out_shape=jax.ShapeDtypeStruct((16, 2 * B), jnp.float32),
        in_specs=[SMEM, SMEM] + [VMEM] * (len(operands) - 2),
        out_specs=VMEM,
        scratch_shapes=[
            pltpu.VMEM((slots, 8, TILE), jnp.float32),
            pltpu.VMEM((slots, 8, TILE), jnp.float32),
            pltpu.VMEM((slots, 32, TILE), jnp.bfloat16),
            pltpu.VMEM((slots, 32, TILE), jnp.bfloat16),
            pltpu.VMEM((3, TILE, TILE), jnp.float32),
            pltpu.VMEM((TILE, 2 * TILE), jnp.bfloat16),
            pltpu.VMEM((TILE, 2 * TILE), jnp.bfloat16),
        ],
        compiler_params=PARAMS,
        name="apply_own" if own else "apply_cross",
    )(*operands)


def boxes(coords, size):
    grouped = coords[0:3].reshape(3, -1, size)
    return jnp.min(grouped, axis=2), jnp.max(grouped, axis=2)


def close_lists(target_box, source_box, flags):
    low_t, high_t = (edge[:, :, None] for edge in target_box)
    low_s, high_s = (edge[:, None, :] for edge in source_box)
    gap = jnp.maximum(jnp.maximum(low_s - high_t, low_t - high_s), 0.0)
    reach = support_radius * support_radius * (1.0 + 1e-4)
    near = jnp.where(jnp.sum(gap * gap, axis=0) <= reach, 1.0, 0.0)
    rows, columns = near.shape
    near = near.reshape(2, rows // 2, flags.shape[1], -1) * flags[:, None, :, None]
    near = near.reshape(rows, columns)
    order = lax.broadcasted_iota(jnp.int32, (columns, columns), 0) <= lax.broadcasted_iota(
        jnp.int32, (columns, columns), 1
    )
    place = jnp.dot(near, order.astype(jnp.float32)).astype(jnp.int32)
    length = columns + BATCH
    wanted = lax.broadcasted_iota(jnp.int32, (rows, length, columns), 1) + 1
    source = lax.broadcasted_iota(jnp.int32, (rows, length, columns), 2)
    match = (place[:, None, :] == wanted) & (near[:, None, :] > 0.0)
    table = jnp.sum(jnp.where(match, source - columns, 0), axis=2) + columns
    return jnp.max(place, axis=1), table


def pair_flags(active, column, count):
    here = lax.dynamic_slice_in_dim(active, column, 1, 0)[0].astype(jnp.float32)
    before = lax.dynamic_slice_in_dim(active, jnp.maximum(column - 1, 0), 1, 0)[0]
    before = before.astype(jnp.float32) * (column >= 1)
    after = here * (column + 1 < count)
    one = jnp.ones((), jnp.float32)
    own = jnp.stack([one, here[0], here[0], one]).reshape(2, 2)
    cross = jnp.stack(
        [before[1], before[3], after[1], after[2], before[2], before[4], after[3], after[4]]
    ).reshape(2, 4)
    return own, cross


def shards(right_side, points, active):
    count = lax.axis_size("blk")
    column = lax.axis_index("blk")
    member = lax.axis_index("rep")
    sides = right_side.shape[0] // lax.axis_size("rep")
    own_flags, cross_flags = pair_flags(active, column, count)

    mine = lax.dynamic_slice_in_dim(right_side, member * sides, sides, 0)
    rows, cols, rank = sort_points(points, mine)
    r0 = rows[0:16]
    around = jnp.concatenate([from_behind(rows, "blk", 1), from_behind(rows, "blk", -1)], axis=1)
    low, high = boxes(rows[16:24], TILE)
    own_lists = close_lists((low, high), boxes(rows[16:24], SUB), own_flags)
    part = apply_pairs(own_lists, cols, rows[16:24], r0)
    cross_lists = close_lists((low, high), boxes(around[16:24], SUB), cross_flags)
    w0 = apply_pairs(cross_lists, cols, around[16:24], around[0:16], part)
    w0_around = jnp.concatenate([from_behind(w0, "blk", 1), from_behind(w0, "blk", -1)], axis=1)
    w0_all = lax.all_gather(unsort(w0, rank), "rep", axis=0, tiled=True)
    part = apply_pairs(own_lists, cols, rows[16:24], w0)
    w1 = apply_pairs(cross_lists, cols, around[16:24], w0_around, part)
    w1_all = lax.all_gather(unsort(w1, rank), "rep", axis=0, tiled=True)

    sums = sum_over_blk(
        jnp.stack([jnp.sum(a * b, axis=1) for a, b in ((r0, r0), (r0, w0), (w0, w0), (w0, w1))])
    )
    s00, s01, s11, s12 = (sums[k] for k in range(4))
    image_norm = shift * s00 + s01
    alpha = s00 / image_norm
    keep = s01 / image_norm
    rr1 = alpha * alpha * (s11 - s01 * (s01 / s00))
    beta = rr1 / s00
    both = keep + beta
    curved = both * both * s01 - 2.0 * both * alpha * s11 + alpha * alpha * s12
    alpha1 = rr1 / (shift * rr1 * (1.0 + beta) + curved)
    factors = jnp.stack(
        [
            (s00 + s01) / image_norm - noise_level * alpha1 * both,
            noise_level * alpha1 * alpha,
            keep - shift * alpha1 * both,
            shift * alpha1 * alpha - alpha - alpha1 * both,
            alpha1 * alpha,
        ]
    )
    spread = jnp.zeros((5, 4, sides), jnp.float32)
    for mask in range(4):
        piece = factors if mask == 0 else exchange(factors, mask, "rep")
        spread = lax.dynamic_update_slice_in_dim(spread, piece[:, None], member ^ mask, 1)
    factor = spread.reshape(5, 4 * sides, 1)
    posterior = factor[0] * right_side + factor[1] * w0_all
    residual = factor[2] * right_side + factor[3] * w0_all + factor[4] * w1_all
    return (posterior, residual)


def solution(mesh):
    return jax.shard_map(
        shards,
        mesh=mesh,
        in_specs=(P(None, "blk"), P(None, "blk"), P()),
        out_specs=(P(None, "blk"), P(None, "blk")),
        check_vma=False,
    )
```

```python
from functools import partial

import jax
import jax.numpy as jnp
from jax import lax
from jax.experimental import pallas as pl
from jax.experimental.pallas import tpu as pltpu
from jax.sharding import PartitionSpec as P

B = 2048
SUB = 64
TILE = 128
STRIP = 256
BATCH = 4
CELLS_X = 4
CELLS_Y = 8
CELLS = CELLS_X * CELLS_Y
FAR = 1.0e6

support_radius = 2.5
noise_level = 8.0
shift = noise_level + 1.0
profile_scale = 4.0 / support_radius**5
VMEM = pl.BlockSpec(memory_space=pltpu.VMEM)
SMEM = pl.BlockSpec(memory_space=pltpu.SMEM)
PARAMS = pltpu.CompilerParams(vmem_limit_bytes=48 * 1024 * 1024)


def from_behind(block, axis, distance):
    devices = range(lax.axis_size(axis))
    route = [(i - distance, i) for i in devices if i - distance in devices]
    return lax.ppermute(block, axis, route)


def exchange(values, mask, axis):
    devices = range(lax.axis_size(axis))
    return lax.ppermute(values, axis, [(i, i ^ mask) for i in devices])


def sum_over_blk(values):
    for base in (1, 4, 16):
        near = values + exchange(values, base, "blk")
        far = exchange(values, 2 * base, "blk") + exchange(values, 3 * base, "blk")
        values = near + far
    return values


def split3(values):
    high = values.astype(jnp.bfloat16)
    rest = values - high.astype(jnp.float32)
    middle = rest.astype(jnp.bfloat16)
    low = (rest - middle.astype(jnp.float32)).astype(jnp.bfloat16)
    return high, middle, low


def one_hot_strip(rank, start):
    place = lax.broadcasted_iota(jnp.int32, (STRIP, B), 0) + start
    return jnp.where(rank == place, 1.0, 0.0).astype(jnp.bfloat16)


def cell_of(values, cells):
    low = jnp.min(values, axis=1, keepdims=True)
    high = jnp.max(values, axis=1, keepdims=True)
    scaled = (values - low) * (cells / jnp.maximum(high - low, 1e-30))
    return jnp.minimum(jnp.floor(scaled), cells - 1.0)


def sort_kernel(
    place_ref,
    points_ref,
    sides_ref,
    rows_ref,
    cols_ref,
    rank_ref,
    box_ref,
    vector_ref,
    feature_ref,
    split_ref,
    edge_ref,
    arrived,
):
    first = pl.multiple_of(place_ref[1] * 16, 16)
    fetch = pltpu.make_async_copy(sides_ref.at[pl.ds(first, 16), :], vector_ref, arrived)
    fetch.start()
    upper = lax.broadcasted_iota(jnp.int32, (TILE, TILE), 0) <= lax.broadcasted_iota(
        jnp.int32, (TILE, TILE), 1
    )
    upper = jnp.where(upper, 1.0, 0.0).astype(jnp.bfloat16)
    lower = lax.broadcasted_iota(jnp.int32, (CELLS, CELLS), 0) > lax.broadcasted_iota(
        jnp.int32, (CELLS, CELLS), 1
    )
    lower = jnp.where(lower, 1.0, 0.0)
    number = lax.broadcasted_iota(jnp.int32, (CELLS, TILE), 0).astype(jnp.float32)
    feature_ref[16:32, :] = jnp.zeros((16, B), jnp.float32)
    split_ref[96:128, :] = jnp.zeros((32, B), jnp.bfloat16)
    for c in range(2):
        span = slice(c * B, (c + 1) * B)
        cell = cell_of(points_ref[0:1, span], CELLS_X) * CELLS_Y + cell_of(
            points_ref[1:2, span], CELLS_Y
        )
        base = jnp.zeros((CELLS, TILE), jnp.float32)
        chosen, place = [], []
        for t in range(B // TILE):
            hit = jnp.where(number == cell[:, t * TILE : (t + 1) * TILE], 1.0, 0.0)
            count = jnp.dot(hit.astype(jnp.bfloat16), upper, preferred_element_type=jnp.float32)
            chosen.append(hit)
            place.append(count + base)
            base = base + count[:, TILE - 1 :]
        offset = jnp.dot(
            lower, base, precision=lax.Precision.HIGHEST, preferred_element_type=jnp.float32
        )
        for t in range(B // TILE):
            rank = jnp.sum(chosen[t] * (place[t] + (offset - 1.0)), axis=0, keepdims=True)
            rank_ref[0:1, c * B + t * TILE : c * B + (t + 1) * TILE] = rank.astype(jnp.int32)
        if c == 0:
            fetch.wait()
        feature_ref[0:16, :] = vector_ref[:, span]
        feature_ref[16:19, :] = points_ref[:, span]
        for k, part in enumerate(split3(feature_ref[...])):
            split_ref[32 * k : 32 * k + 32, :] = part
        rank = rank_ref[0:1, span]
        for k in range(B // STRIP):
            found = lax.dot_general(
                one_hot_strip(rank, k * STRIP),
                split_ref[...],
                (((1,), (1,)), ((), ())),
                preferred_element_type=jnp.float32,
            )
            found = found + pltpu.roll(found, 96, 1) + pltpu.roll(found, 64, 1)
            spot = slice(c * B + k * STRIP, c * B + (k + 1) * STRIP)
            cols_ref[spot, :] = found
            rows_ref[:, spot] = found.T[0:24, :]
            for t in range(STRIP // SUB):
                chunk = c * (B // SUB) + k * (STRIP // SUB) + t
                piece = found[t * SUB : (t + 1) * SUB, :]
                for e, edge in enumerate((jnp.min, jnp.max)):
                    value = edge(piece, axis=0, keepdims=True)
                    edge_ref[e, chunk : chunk + 1, :] = value
                    edge_ref[e, 64 + chunk : 65 + chunk, :] = value
            for t in range(STRIP // TILE):
                j = c * (B // TILE) + k * (STRIP // TILE) + t
                piece = found[t * TILE : (t + 1) * TILE, :]
                for e, edge in enumerate((jnp.min, jnp.max)):
                    box_ref[e, j : j + 1, :] = edge(piece, axis=0, keepdims=True)
    for e in range(2):
        turned = edge_ref[e].T
        for axis in range(3):
            rows_ref[19 + e : 20 + e, axis * TILE : (axis + 1) * TILE] = turned[
                16 + axis : 17 + axis, :
            ]


def sort_points(place, points, right_side):
    width = 2 * B
    return pl.pallas_call(
        sort_kernel,
        out_shape=(
            jax.ShapeDtypeStruct((24, width), jnp.float32),
            jax.ShapeDtypeStruct((width, TILE), jnp.float32),
            jax.ShapeDtypeStruct((8, width), jnp.int32),
            jax.ShapeDtypeStruct((2, width // TILE, TILE), jnp.float32),
        ),
        in_specs=[SMEM, VMEM, pl.BlockSpec(memory_space=pl.ANY)],
        out_specs=(VMEM, VMEM, VMEM, VMEM),
        scratch_shapes=[
            pltpu.VMEM((16, width), jnp.float32),
            pltpu.VMEM((32, B), jnp.float32),
            pltpu.VMEM((128, B), jnp.bfloat16),
            pltpu.VMEM((2, TILE, TILE), jnp.float32),
            pltpu.SemaphoreType.DMA,
        ],
        compiler_params=PARAMS,
        name="sort_points",
    )(place, points, right_side)


def unsort_kernel(sorted_ref, rank_ref, out_ref, split_ref, total_ref):
    for c in range(2):
        span = slice(c * B, (c + 1) * B)
        for k, part in enumerate(split3(sorted_ref[:, span])):
            split_ref[16 * k : 16 * k + 16, :] = part
        rank = rank_ref[0:1, span]
        for k in range(B // STRIP):
            found = jnp.dot(
                split_ref[:, k * STRIP : (k + 1) * STRIP],
                one_hot_strip(rank, k * STRIP),
                preferred_element_type=jnp.float32,
            )
            total_ref[...] = found if k == 0 else total_ref[...] + found
        out_ref[:, span] = (total_ref[0:16, :] + total_ref[16:32, :]) + total_ref[32:48, :]


def unsort(values, rank):
    return pl.pallas_call(
        unsort_kernel,
        out_shape=jax.ShapeDtypeStruct(values.shape, jnp.float32),
        in_specs=[VMEM, VMEM],
        out_specs=VMEM,
        scratch_shapes=[pltpu.VMEM((48, B), jnp.bfloat16), pltpu.VMEM((48, B), jnp.float32)],
        compiler_params=PARAMS,
        name="unsort",
    )(values, rank)


def pair_table(own, place_ref, active_ref, box_ref, xyz_refs, null):
    shape = (box_ref.shape[1], TILE)
    row = lax.broadcasted_iota(jnp.int32, shape, 0)
    lane = lax.broadcasted_iota(jnp.int32, shape, 1)
    total = jnp.zeros(shape, jnp.float32)
    for axis in range(3):
        low_t = box_ref[0, :, 16 + axis : 17 + axis]
        high_t = box_ref[1, :, 16 + axis : 17 + axis]
        span = slice(axis * TILE, (axis + 1) * TILE)
        edges = [[ref[19 + e : 20 + e, span] for e in range(2)] for ref in xyz_refs]
        if own:
            low_s, high_s = edges[0]
        else:
            is_before = lane[0:1] < SUB
            low_s, high_s = (jnp.where(is_before, edges[0][e], edges[1][e]) for e in range(2))
        gap = jnp.maximum(jnp.maximum(low_s - high_t, low_t - high_s), 0.0)
        total = total + gap * gap
    near = total <= support_radius * support_radius * (1.0 + 1e-4)
    column = place_ref[0]
    count = active_ref.shape[0]
    is_second = row >= shape[0] // 2
    quarter = lane // (TILE // 4)
    if own:
        across = active_ref[column, 0]
        same = is_second == (quarter == 1)
        flag = jnp.where(same, 1, across)
        flag = jnp.where(quarter < 2, flag, 0)
    else:
        behind = jnp.maximum(column - 1, 0)
        has_behind = jnp.where(column >= 1, 1, 0)
        has_ahead = jnp.where(column + 1 < count, 1, 0)
        flag = jnp.zeros(shape, jnp.int32)
        for c in range(2):
            for q in range(4):
                if q < 2:
                    value = active_ref[behind, 1 + 2 * q + c] * has_behind
                else:
                    value = active_ref[column, 1 + 2 * c + (q - 2)] * has_ahead
                here = (is_second == (c == 1)) & (quarter == q)
                flag = jnp.where(here, value, flag)
    near = near & (flag > 0)
    upper = lax.broadcasted_iota(jnp.int32, (TILE, TILE), 0) <= lax.broadcasted_iota(
        jnp.int32, (TILE, TILE), 1
    )
    place = jnp.dot(
        jnp.where(near, 1.0, 0.0).astype(jnp.bfloat16),
        jnp.where(upper, 1.0, 0.0).astype(jnp.bfloat16),
        preferred_element_type=jnp.float32,
    ).astype(jnp.int32)
    value = jnp.where(near, lane, null)
    left = jnp.where(near, lane + 1 - place, 0)
    for bit in range(7):
        amount = 1 << bit
        next_value = pltpu.roll(value, TILE - amount, 1)
        next_left = pltpu.roll(left, TILE - amount, 1)
        arrives = (next_left & amount) > 0
        stays = (left & amount) == 0
        value = jnp.where(arrives, next_value, jnp.where(stays, value, null))
        left = jnp.where(arrives, next_left, jnp.where(stays, left, 0))
    return value + 256 * place[:, TILE - 1 :]


def apply_kernel(own, sums, *refs):
    refs = list(refs)
    place_ref, active_ref, cols_ref, box_ref = refs[:4]
    del refs[:4]
    sources = 1 if own else 2
    xyz_refs = [refs.pop(0) for _ in range(sources)]
    vec_refs = [refs.pop(0) for _ in range(sources)]
    add_ref = None if own else refs.pop(0)
    base_refs = [refs.pop(0) for _ in range(2)] if sums else None
    out_ref = refs.pop(0)
    sums_ref = refs.pop(0) if sums else None
    left_xyz, right_xyz, left_w, right_w, target, tiles, weights, total_ref = refs[:8]
    table_ref, list_ref, arrived = refs[8:]
    rows = out_ref.shape[1] // TILE
    null = 2 * rows * sources
    lane = lax.broadcasted_iota(jnp.int32, (8, TILE), 1)
    is_left = lane < SUB

    table_ref[...] = pair_table(own, place_ref, active_ref, box_ref, xyz_refs, null)
    load = pltpu.make_async_copy(table_ref, list_ref, arrived)
    load.start()

    def spread(values):
        turned = pltpu.roll(values, SUB, 1)
        mask = jnp.concatenate([is_left] * (values.shape[0] // 8), axis=0)
        zero = jnp.zeros_like(values)
        return (
            jnp.where(mask, values, zero),
            jnp.where(mask, zero, turned),
            jnp.where(mask, turned, zero),
            jnp.where(mask, zero, values),
        )

    def parts(values):
        high = values.astype(jnp.bfloat16)
        low = (values - high.astype(jnp.float32)).astype(jnp.bfloat16)
        return jnp.concatenate([high, low], axis=0)

    for s in range(sources):

        def prepare(g, carry):
            for u in range(4):
                t = g * 4 + u
                spot = pl.ds(pl.multiple_of(t * TILE, TILE), TILE)
                slot = 2 * (t + s * rows)
                xyz = spread(xyz_refs[s][16:24, spot])
                left_xyz[slot] = xyz[0]
                right_xyz[slot] = xyz[1]
                left_xyz[slot + 1] = xyz[2]
                right_xyz[slot + 1] = xyz[3]
                vec = spread(vec_refs[s][0:16, spot])
                left_w[slot] = parts(vec[0])
                right_w[slot] = parts(vec[1])
                left_w[slot + 1] = parts(vec[2])
                right_w[slot + 1] = parts(vec[3])
            return carry

        lax.fori_loop(0, rows // 4, prepare, 0)
    left_xyz[null] = jnp.where(is_left, FAR, 0.0)
    right_xyz[null] = jnp.where(is_left, 0.0, FAR)
    left_w[null] = jnp.zeros((32, TILE), jnp.bfloat16)
    right_w[null] = jnp.zeros((32, TILE), jnp.bfloat16)
    total_ref[...] = jnp.zeros_like(total_ref)
    tiles[1] = jnp.zeros((TILE, 4 * TILE), jnp.bfloat16)
    weights[1] = jnp.zeros((32, 4 * TILE), jnp.bfloat16)

    def form(side, j, n):
        for s in range(2):
            first = list_ref[j, 4 * n + 2 * s] & 255
            second = list_ref[j, 4 * n + 2 * s + 1] & 255
            xyz = left_xyz[first] + right_xyz[second]
            weight = left_w[first] + right_w[second]
            near = slice(2 * s * TILE, (2 * s + 1) * TILE)
            far = slice((2 * s + 1) * TILE, (2 * s + 2) * TILE)
            weights[side, :, near] = weight
            weights[side, :, far] = weight
            for r in range(TILE // 16):
                span = slice(16 * r, 16 * r + 16)
                dx = target[3 * side, span, :] - xyz[0:1, :]
                dy = target[3 * side + 1, span, :] - xyz[1:2, :]
                dz = target[3 * side + 2, span, :] - xyz[2:3, :]
                square = jnp.maximum(dx * dx + dy * dy + dz * dz, 1e-30)
                distance = square * lax.rsqrt(square)
                inside = jnp.maximum(support_radius - distance, 0.0)
                inside = inside * inside
                value = (inside * inside) * (distance + 0.25 * support_radius)
                high = value.astype(jnp.bfloat16)
                tiles[side, span, near] = high
                tiles[side, span, far] = (value - high.astype(jnp.float32)).astype(jnp.bfloat16)

    def apply(side):
        return lax.dot_general(
            weights[side],
            tiles[side],
            (((1,), (1,)), ((), ())),
            preferred_element_type=jnp.float32,
        )

    load.wait()

    def row_pair(j, last):
        other = rows - 1 - j
        count = jnp.maximum(list_ref[j, 0], list_ref[other, 0]) // 256

        @pl.when(count > 0)
        def _():
            for side, k in enumerate((j, other)):
                spot = pl.ds(pl.multiple_of(k * TILE, TILE), TILE)
                for axis in range(3):
                    target[3 * side + axis] = jnp.broadcast_to(
                        cols_ref[spot, 16 + axis : 17 + axis], (TILE, TILE)
                    )

        def step(n, last):
            image = apply(1)
            form(0, j, n)
            total_ref[last] += image
            image = apply(0)
            form(1, other, n)
            total_ref[j] += image
            return other

        return lax.fori_loop(0, (count + BATCH - 1) // BATCH, step, last)

    last = lax.fori_loop(0, rows // 2, row_pair, 0)
    total_ref[last] += apply(1)

    def finish(g, running):
        for u in range(4):
            j = g * 4 + u
            spot = pl.ds(pl.multiple_of(j * TILE, TILE), TILE)
            total = total_ref[j]
            image = (total[0:16, :] + total[16:32, :]) * profile_scale
            if own:
                held = (left_w[2 * j] + right_w[2 * j + 1]).astype(jnp.float32)
                image = image - (held[0:16, :] + held[16:32, :])
            else:
                image = image + add_ref[:, spot]
            out_ref[:, spot] = image
            if sums:
                side = base_refs[0][0:16, spot]
                first = base_refs[1][:, spot]
                running = (
                    running[0] + side * side,
                    running[1] + side * first,
                    running[2] + first * first,
                    running[3] + first * image,
                )
        return running

    zero = jnp.zeros((16, TILE), jnp.float32)
    result = lax.fori_loop(0, rows // 4, finish, (zero,) * 4 if sums else 0)
    if sums:
        columns = lax.broadcasted_iota(jnp.int32, (16, TILE), 1)
        packed = zero
        for k in range(4):
            packed = jnp.where(columns == k, jnp.sum(result[k], axis=1, keepdims=True), packed)
        sums_ref[...] = packed


def apply_pairs(place, active, cols, box, coords, vectors, added=None, bases=()):
    own = added is None
    sums = bool(bases)
    operands = [place, active, cols, box, *coords, *vectors]
    operands += ([] if own else [added]) + list(bases)
    rows = 2 * B // TILE
    slots = 2 * rows * len(coords) + 1
    out_shape = [jax.ShapeDtypeStruct((16, 2 * B), jnp.float32)]
    if sums:
        out_shape.append(jax.ShapeDtypeStruct((16, TILE), jnp.float32))
    result = pl.pallas_call(
        partial(apply_kernel, own, sums),
        out_shape=out_shape,
        in_specs=[SMEM, SMEM] + [VMEM] * (len(operands) - 2),
        out_specs=[VMEM] * len(out_shape),
        scratch_shapes=[
            pltpu.VMEM((slots, 8, TILE), jnp.float32),
            pltpu.VMEM((slots, 8, TILE), jnp.float32),
            pltpu.VMEM((slots, 32, TILE), jnp.bfloat16),
            pltpu.VMEM((slots, 32, TILE), jnp.bfloat16),
            pltpu.VMEM((6, TILE, TILE), jnp.float32),
            pltpu.VMEM((2, TILE, 4 * TILE), jnp.bfloat16),
            pltpu.VMEM((2, 32, 4 * TILE), jnp.bfloat16),
            pltpu.VMEM((rows, 32, TILE), jnp.float32),
            pltpu.VMEM((rows, TILE), jnp.int32),
            pltpu.SMEM((rows, TILE), jnp.int32),
            pltpu.SemaphoreType.DMA,
        ],
        compiler_params=PARAMS,
        name="apply_own" if own else "apply_cross",
    )(*operands)
    return result if sums else result[0]


def shards(right_side, points, active):
    column = lax.axis_index("blk")
    member = lax.axis_index("rep")
    sides = right_side.shape[0] // lax.axis_size("rep")
    place = jnp.stack([column, member]).astype(jnp.int32)

    def neighbours(values):
        return from_behind(values, "blk", 1), from_behind(values, "blk", -1)

    rows, cols, rank, box = sort_points(place, points, right_side)
    around = neighbours(rows)
    fixed = (place, active, cols, box)
    part = apply_pairs(*fixed, (rows,), (rows,))
    w0 = apply_pairs(*fixed, around, around, part)
    w0_around = neighbours(w0)
    w0_all = lax.all_gather(unsort(w0, rank), "rep", axis=0, tiled=True)
    part = apply_pairs(*fixed, (rows,), (w0,))
    w1, sums = apply_pairs(*fixed, around, w0_around, part, (rows, w0))
    w1_all = lax.all_gather(unsort(w1, rank), "rep", axis=0, tiled=True)
    sums = sum_over_blk(sums[:, 0:4].T)
    s00, s01, s11, s12 = (sums[k] for k in range(4))
    image_norm = shift * s00 + s01
    alpha = s00 / image_norm
    keep = s01 / image_norm
    rr1 = alpha * alpha * (s11 - s01 * (s01 / s00))
    beta = rr1 / s00
    both = keep + beta
    curved = both * both * s01 - 2.0 * both * alpha * s11 + alpha * alpha * s12
    alpha1 = rr1 / (shift * rr1 * (1.0 + beta) + curved)
    factors = jnp.stack(
        [
            (s00 + s01) / image_norm - noise_level * alpha1 * both,
            noise_level * alpha1 * alpha,
            keep - shift * alpha1 * both,
            shift * alpha1 * alpha - alpha - alpha1 * both,
            alpha1 * alpha,
        ]
    )
    spread = jnp.zeros((5, 4, sides), jnp.float32)
    for mask in range(4):
        piece = factors if mask == 0 else exchange(factors, mask, "rep")
        spread = lax.dynamic_update_slice_in_dim(spread, piece[:, None], member ^ mask, 1)
    factor = spread.reshape(5, 4 * sides, 1)
    posterior = factor[0] * right_side + factor[1] * w0_all
    residual = factor[2] * right_side + factor[3] * w0_all + factor[4] * w1_all
    return (posterior, residual)


def solution(mesh):
    return jax.shard_map(
        shards,
        mesh=mesh,
        in_specs=(P(None, "blk"), P(None, "blk"), P()),
        out_specs=(P(None, "blk"), P(None, "blk")),
        check_vma=False,
    )
```

```python
from functools import partial

import jax
import jax.numpy as jnp
from jax import lax
from jax.experimental import pallas as pl
from jax.experimental.pallas import tpu as pltpu
from jax.sharding import PartitionSpec as P

B = 2048
SUB = 64
TILE = 128
STRIP = 256
BATCH = 4
GROUP = 4
KEPT = {True: 32, False: 8}
CELLS_X = 4
CELLS_Y = 8
CELLS = CELLS_X * CELLS_Y
FAR = 1.0e6

support_radius = 2.5
noise_level = 8.0
shift = noise_level + 1.0
profile_scale = 4.0 / support_radius**5
VMEM = pl.BlockSpec(memory_space=pltpu.VMEM)
SMEM = pl.BlockSpec(memory_space=pltpu.SMEM)
PARAMS = pltpu.CompilerParams(vmem_limit_bytes=48 * 1024 * 1024)


def from_behind(block, axis, distance):
    devices = range(lax.axis_size(axis))
    route = [(i - distance, i) for i in devices if i - distance in devices]
    return lax.ppermute(block, axis, route)


def split3(values):
    high = values.astype(jnp.bfloat16)
    rest = values - high.astype(jnp.float32)
    middle = rest.astype(jnp.bfloat16)
    low = (rest - middle.astype(jnp.float32)).astype(jnp.bfloat16)
    return high, middle, low


def one_hot_strip(rank, start):
    place = lax.broadcasted_iota(jnp.int32, (STRIP, B), 0) + start
    return jnp.where(rank == place, 1.0, 0.0).astype(jnp.bfloat16)


def cell_of(values, cells):
    low = jnp.min(values, axis=1, keepdims=True)
    high = jnp.max(values, axis=1, keepdims=True)
    scaled = (values - low) * (cells / jnp.maximum(high - low, 1e-30))
    return jnp.minimum(jnp.floor(scaled), cells - 1.0)


def sort_kernel(
    place_ref,
    points_ref,
    sides_ref,
    rows_ref,
    cols_ref,
    rank_ref,
    box_ref,
    vector_ref,
    feature_ref,
    split_ref,
    edge_ref,
    arrived,
):
    first = pl.multiple_of(place_ref[1] * 16, 16)
    fetch = pltpu.make_async_copy(sides_ref.at[pl.ds(first, 16), :], vector_ref, arrived)
    fetch.start()
    upper = lax.broadcasted_iota(jnp.int32, (TILE, TILE), 0) <= lax.broadcasted_iota(
        jnp.int32, (TILE, TILE), 1
    )
    upper = jnp.where(upper, 1.0, 0.0).astype(jnp.bfloat16)
    lower = lax.broadcasted_iota(jnp.int32, (CELLS, CELLS), 0) > lax.broadcasted_iota(
        jnp.int32, (CELLS, CELLS), 1
    )
    lower = jnp.where(lower, 1.0, 0.0)
    number = lax.broadcasted_iota(jnp.int32, (CELLS, TILE), 0).astype(jnp.float32)
    feature_ref[16:32, :] = jnp.zeros((16, B), jnp.float32)
    split_ref[96:128, :] = jnp.zeros((32, B), jnp.bfloat16)
    for c in range(2):
        span = slice(c * B, (c + 1) * B)
        cell = cell_of(points_ref[0:1, span], CELLS_X) * CELLS_Y + cell_of(
            points_ref[1:2, span], CELLS_Y
        )
        base = jnp.zeros((CELLS, TILE), jnp.float32)
        chosen, place = [], []
        for t in range(B // TILE):
            hit = jnp.where(number == cell[:, t * TILE : (t + 1) * TILE], 1.0, 0.0)
            count = jnp.dot(hit.astype(jnp.bfloat16), upper, preferred_element_type=jnp.float32)
            chosen.append(hit)
            place.append(count + base)
            base = base + count[:, TILE - 1 :]
        offset = jnp.dot(
            lower, base, precision=lax.Precision.HIGHEST, preferred_element_type=jnp.float32
        )
        for t in range(B // TILE):
            rank = jnp.sum(chosen[t] * (place[t] + (offset - 1.0)), axis=0, keepdims=True)
            rank_ref[0:1, c * B + t * TILE : c * B + (t + 1) * TILE] = rank.astype(jnp.int32)
        if c == 0:
            fetch.wait()
        feature_ref[0:16, :] = vector_ref[:, span]
        feature_ref[16:19, :] = points_ref[:, span]
        for k, part in enumerate(split3(feature_ref[...])):
            split_ref[32 * k : 32 * k + 32, :] = part
        rank = rank_ref[0:1, span]
        for k in range(B // STRIP):
            found = lax.dot_general(
                one_hot_strip(rank, k * STRIP),
                split_ref[...],
                (((1,), (1,)), ((), ())),
                preferred_element_type=jnp.float32,
            )
            found = found + pltpu.roll(found, 96, 1) + pltpu.roll(found, 64, 1)
            spot = slice(c * B + k * STRIP, c * B + (k + 1) * STRIP)
            cols_ref[spot, :] = found
            rows_ref[:, spot] = found.T[0:24, :]
            for t in range(STRIP // SUB):
                chunk = c * (B // SUB) + k * (STRIP // SUB) + t
                piece = found[t * SUB : (t + 1) * SUB, :]
                for e, edge in enumerate((jnp.min, jnp.max)):
                    value = edge(piece, axis=0, keepdims=True)
                    edge_ref[e, chunk : chunk + 1, :] = value
                    edge_ref[e, 64 + chunk : 65 + chunk, :] = value
            for t in range(STRIP // TILE):
                j = c * (B // TILE) + k * (STRIP // TILE) + t
                piece = found[t * TILE : (t + 1) * TILE, :]
                for e, edge in enumerate((jnp.min, jnp.max)):
                    box_ref[e, j : j + 1, :] = edge(piece, axis=0, keepdims=True)
    for e in range(2):
        turned = edge_ref[e].T
        for axis in range(3):
            rows_ref[19 + e : 20 + e, axis * TILE : (axis + 1) * TILE] = turned[
                16 + axis : 17 + axis, :
            ]


def sort_points(place, points, right_side):
    width = 2 * B
    return pl.pallas_call(
        sort_kernel,
        out_shape=(
            jax.ShapeDtypeStruct((24, width), jnp.float32),
            jax.ShapeDtypeStruct((width, TILE), jnp.float32),
            jax.ShapeDtypeStruct((8, width), jnp.int32),
            jax.ShapeDtypeStruct((2, width // TILE, TILE), jnp.float32),
        ),
        in_specs=[SMEM, VMEM, pl.BlockSpec(memory_space=pl.ANY)],
        out_specs=(VMEM, VMEM, VMEM, VMEM),
        scratch_shapes=[
            pltpu.VMEM((16, width), jnp.float32),
            pltpu.VMEM((32, B), jnp.float32),
            pltpu.VMEM((128, B), jnp.bfloat16),
            pltpu.VMEM((2, TILE, TILE), jnp.float32),
            pltpu.SemaphoreType.DMA,
        ],
        compiler_params=PARAMS,
        name="sort_points",
    )(place, points, right_side)


def unsort_kernel(sorted_ref, rank_ref, out_ref, split_ref, total_ref):
    for c in range(2):
        span = slice(c * B, (c + 1) * B)
        for k, part in enumerate(split3(sorted_ref[:, span])):
            split_ref[16 * k : 16 * k + 16, :] = part
        rank = rank_ref[0:1, span]
        for k in range(B // STRIP):
            found = jnp.dot(
                split_ref[:, k * STRIP : (k + 1) * STRIP],
                one_hot_strip(rank, k * STRIP),
                preferred_element_type=jnp.float32,
            )
            total_ref[...] = found if k == 0 else total_ref[...] + found
        out_ref[:, span] = (total_ref[0:16, :] + total_ref[16:32, :]) + total_ref[32:48, :]


def unsort(values, rank):
    return pl.pallas_call(
        unsort_kernel,
        out_shape=jax.ShapeDtypeStruct(values.shape, jnp.float32),
        in_specs=[VMEM, VMEM],
        out_specs=VMEM,
        scratch_shapes=[pltpu.VMEM((48, B), jnp.bfloat16), pltpu.VMEM((48, B), jnp.float32)],
        compiler_params=PARAMS,
        name="unsort",
    )(values, rank)


def pair_table(own, place_ref, active_ref, box_ref, xyz_refs, null):
    shape = (box_ref.shape[1], TILE)
    row = lax.broadcasted_iota(jnp.int32, shape, 0)
    lane = lax.broadcasted_iota(jnp.int32, shape, 1)
    total = jnp.zeros(shape, jnp.float32)
    for axis in range(3):
        low_t = box_ref[0, :, 16 + axis : 17 + axis]
        high_t = box_ref[1, :, 16 + axis : 17 + axis]
        span = slice(axis * TILE, (axis + 1) * TILE)
        edges = [[ref[19 + e : 20 + e, span] for e in range(2)] for ref in xyz_refs]
        if own:
            low_s, high_s = edges[0]
        else:
            is_before = lane[0:1] < SUB
            low_s, high_s = (jnp.where(is_before, edges[0][e], edges[1][e]) for e in range(2))
        gap = jnp.maximum(jnp.maximum(low_s - high_t, low_t - high_s), 0.0)
        total = total + gap * gap
    near = total <= support_radius * support_radius * (1.0 + 1e-4)
    column = place_ref[0]
    count = active_ref.shape[0]
    is_second = row >= shape[0] // 2
    quarter = lane // (TILE // 4)
    if own:
        across = active_ref[column, 0]
        same = is_second == (quarter == 1)
        flag = jnp.where(same, 1, across)
        flag = jnp.where(quarter < 2, flag, 0)
    else:
        behind = jnp.maximum(column - 1, 0)
        has_behind = jnp.where(column >= 1, 1, 0)
        has_ahead = jnp.where(column + 1 < count, 1, 0)
        flag = jnp.zeros(shape, jnp.int32)
        for c in range(2):
            for q in range(4):
                if q < 2:
                    value = active_ref[behind, 1 + 2 * q + c] * has_behind
                else:
                    value = active_ref[column, 1 + 2 * c + (q - 2)] * has_ahead
                here = (is_second == (c == 1)) & (quarter == q)
                flag = jnp.where(here, value, flag)
    near = near & (flag > 0)
    upper = lax.broadcasted_iota(jnp.int32, (TILE, TILE), 0) <= lax.broadcasted_iota(
        jnp.int32, (TILE, TILE), 1
    )
    place = jnp.dot(
        jnp.where(near, 1.0, 0.0).astype(jnp.bfloat16),
        jnp.where(upper, 1.0, 0.0).astype(jnp.bfloat16),
        preferred_element_type=jnp.float32,
    ).astype(jnp.int32)
    value = jnp.where(near, lane, null)
    left = jnp.where(near, lane + 1 - place, 0)
    for bit in range(7):
        amount = 1 << bit
        next_value = pltpu.roll(value, TILE - amount, 1)
        next_left = pltpu.roll(left, TILE - amount, 1)
        arrives = (next_left & amount) > 0
        stays = (left & amount) == 0
        value = jnp.where(arrives, next_value, jnp.where(stays, value, null))
        left = jnp.where(arrives, next_left, jnp.where(stays, left, 0))
    return value + 256 * place[:, TILE - 1 :]


def apply_kernel(own, again, *refs):
    refs = list(refs)
    place_ref, active_ref, cols_ref, box_ref = refs[:4]
    del refs[:4]
    sources = 1 if own else 2
    xyz_refs = [refs.pop(0) for _ in range(sources)]
    vec_refs = [refs.pop(0) for _ in range(sources)]
    add_ref = None if own else refs.pop(0)
    sums = again and not own
    base_refs = [refs.pop(0) for _ in range(2)] if sums else None
    kept_ref = refs.pop(0) if again else None
    out_ref = refs.pop(0)
    if not again:
        kept_ref = refs.pop(0)
    sums_ref = refs.pop(0) if sums else None
    left_xyz, right_xyz, left_w, right_w, target, bank, weights, total_ref = refs[:8]
    table_ref, list_ref, arrived, moved = refs[8:]
    rows = out_ref.shape[1] // TILE
    cells = rows // GROUP
    kept = KEPT[own]
    null = 2 * rows * sources
    lane = lax.broadcasted_iota(jnp.int32, (8, TILE), 1)
    is_left = lane < SUB

    table_ref[...] = pair_table(own, place_ref, active_ref, box_ref, xyz_refs, null)
    load = pltpu.make_async_copy(table_ref, list_ref, arrived)
    load.start()

    def spread(values):
        turned = pltpu.roll(values, SUB, 1)
        mask = jnp.concatenate([is_left] * (values.shape[0] // 8), axis=0)
        zero = jnp.zeros_like(values)
        return (
            jnp.where(mask, values, zero),
            jnp.where(mask, zero, turned),
            jnp.where(mask, turned, zero),
            jnp.where(mask, zero, values),
        )

    def parts(values):
        high = values.astype(jnp.bfloat16)
        low = (values - high.astype(jnp.float32)).astype(jnp.bfloat16)
        return jnp.concatenate([high, low], axis=0)

    for s in range(sources):

        def prepare(g, carry):
            for u in range(4):
                t = g * 4 + u
                spot = pl.ds(pl.multiple_of(t * TILE, TILE), TILE)
                slot = 2 * (t + s * rows)
                xyz = spread(xyz_refs[s][16:24, spot])
                left_xyz[slot] = xyz[0]
                right_xyz[slot] = xyz[1]
                left_xyz[slot + 1] = xyz[2]
                right_xyz[slot + 1] = xyz[3]
                vec = spread(vec_refs[s][0:16, spot])
                left_w[slot] = parts(vec[0])
                right_w[slot] = parts(vec[1])
                left_w[slot + 1] = parts(vec[2])
                right_w[slot + 1] = parts(vec[3])
            return carry

        lax.fori_loop(0, rows // 4, prepare, 0)
    left_xyz[null] = jnp.where(is_left, FAR, 0.0)
    right_xyz[null] = jnp.where(is_left, 0.0, FAR)
    left_w[null] = jnp.zeros((32, TILE), jnp.bfloat16)
    right_w[null] = jnp.zeros((32, TILE), jnp.bfloat16)
    total_ref[...] = jnp.zeros_like(total_ref)
    bank[kept] = jnp.zeros(bank.shape[1:], jnp.bfloat16)
    weights[...] = jnp.zeros_like(weights)

    def members(cell):
        mirror = cell + 3 * cells // 2 - cells * (cell // (cells // 2))
        return cell, mirror, rows - 1 - mirror, rows - 1 - cell

    def batches(cell):
        count = list_ref[cell, 0]
        for j in members(cell)[1:]:
            count = jnp.maximum(count, list_ref[j, 0])
        return (count // 256 + BATCH - 1) // BATCH

    def aim(cell):
        for k, j in enumerate(members(cell)):
            spot = pl.ds(pl.multiple_of(j * TILE, TILE), TILE)
            for axis in range(3):
                target[3 * k + axis] = jnp.broadcast_to(
                    cols_ref[spot, 16 + axis : 17 + axis], (TILE, TILE)
                )

    def chunks(j, n, s):
        return list_ref[j, 4 * n + 2 * s] & 255, list_ref[j, 4 * n + 2 * s + 1] & 255

    def weigh(k, j, n):
        for s in range(2):
            first, second = chunks(j, n, s)
            weights[k, :, s * TILE : (s + 1) * TILE] = left_w[first] + right_w[second]

    def form(slot, k, j, n):
        for s in range(2):
            first, second = chunks(j, n, s)
            xyz = left_xyz[first] + right_xyz[second]
            here = slice(s * TILE, (s + 1) * TILE)
            for r in range(TILE // 16):
                span = slice(16 * r, 16 * r + 16)
                dx = target[3 * k, span, :] - xyz[0:1, :]
                dy = target[3 * k + 1, span, :] - xyz[1:2, :]
                dz = target[3 * k + 2, span, :] - xyz[2:3, :]
                square = jnp.maximum(dx * dx + dy * dy + dz * dz, 1e-30)
                distance = square * lax.rsqrt(square)
                inside = jnp.maximum(support_radius - distance, 0.0)
                inside = inside * inside
                value = (inside * inside) * (distance + 0.25 * support_radius)
                high = value.astype(jnp.bfloat16)
                low = (value - high.astype(jnp.float32)).astype(jnp.bfloat16)
                bank[slot, k, 16 * r : 16 * r + 16, here] = high
                bank[slot, k, TILE + 16 * r : TILE + 16 * r + 16, here] = low

    def apply(slot, k):
        both = lax.dot_general(
            weights[k],
            bank[slot, k],
            (((1,), (1,)), ((), ())),
            preferred_element_type=jnp.float32,
        )
        return both[:, 0:TILE] + both[:, TILE : 2 * TILE]

    def add(cell, images):
        for j, image in zip(members(cell), images):
            total_ref[j] += image

    def transfer(g):
        ends = (kept_ref.at[g], bank.at[g]) if again else (bank.at[g], kept_ref.at[g])
        return pltpu.make_async_copy(*ends, moved.at[g])

    load.wait()
    used = lax.fori_loop(0, cells, lambda cell, n: n + batches(cell), 0)
    used = jnp.minimum(used, kept)

    if again:
        lax.fori_loop(0, used, lambda g, carry: (transfer(g).start(), carry)[1], 0)

        def row_group(cell, g):
            def step(n, g):
                slot = jnp.minimum(g, kept)

                @pl.when(g < kept)
                def _():
                    transfer(g).wait()

                @pl.when(g >= kept)
                def _():
                    aim(cell)
                    for k, j in enumerate(members(cell)):
                        form(slot, k, j, n)

                for k, j in enumerate(members(cell)):
                    weigh(k, j, n)
                add(cell, [apply(slot, k) for k in range(GROUP)])
                return g + 1

            return lax.fori_loop(0, batches(cell), step, g)

        lax.fori_loop(0, cells, row_group, 0)
    else:

        def row_group(cell, state):
            count = batches(cell)

            @pl.when(count > 0)
            def _():
                aim(cell)

            def step(n, state):
                g, last_slot, last_cell = state
                slot = jnp.minimum(g, kept)
                images = [apply(last_slot, k) for k in range(GROUP)]
                for k, j in enumerate(members(cell)):
                    weigh(k, j, n)
                    form(slot, k, j, n)
                add(last_cell, images)

                @pl.when(g < kept)
                def _():
                    transfer(g).start()

                return g + 1, slot, cell

            return lax.fori_loop(0, count, step, state)

        _, slot, cell = lax.fori_loop(0, cells, row_group, (0, kept, 0))
        add(cell, [apply(slot, k) for k in range(GROUP)])

    def finish(g, running):
        for u in range(4):
            j = g * 4 + u
            spot = pl.ds(pl.multiple_of(j * TILE, TILE), TILE)
            total = total_ref[j]
            image = (total[0:16, :] + total[16:32, :]) * profile_scale
            if own:
                held = (left_w[2 * j] + right_w[2 * j + 1]).astype(jnp.float32)
                image = image - (held[0:16, :] + held[16:32, :])
            else:
                image = image + add_ref[:, spot]
            out_ref[:, spot] = image
            if sums:
                side = base_refs[0][0:16, spot]
                first = base_refs[1][:, spot]
                running = (
                    running[0] + side * side,
                    running[1] + side * first,
                    running[2] + first * first,
                    running[3] + first * image,
                )
        return running

    zero = jnp.zeros((16, TILE), jnp.float32)
    result = lax.fori_loop(0, rows // 4, finish, (zero,) * 4 if sums else 0)
    if not again:
        lax.fori_loop(0, used, lambda g, carry: (transfer(g).wait(), carry)[1], 0)
    if sums:
        columns = lax.broadcasted_iota(jnp.int32, (16, TILE), 1)
        packed = zero
        for k in range(4):
            packed = jnp.where(columns == k, jnp.sum(result[k], axis=1, keepdims=True), packed)
        turned = jnp.concatenate([packed] + [zero] * 7, axis=0).T
        line = turned[0:1]
        for k in range(1, 4):
            line = line + pltpu.roll(turned[k : k + 1], 16 * k, 1)
        sums_ref[...] = jnp.broadcast_to(line, sums_ref.shape)


def apply_pairs(fixed, coords, vectors, added=None, bases=(), kept=None):
    own = added is None
    again = kept is not None
    operands = [*fixed, *coords, *vectors]
    operands += ([] if own else [added]) + list(bases)
    specs = [SMEM, SMEM] + [VMEM] * (len(operands) - 2)
    rows = 2 * B // TILE
    slots = 2 * rows * len(coords) + 1
    out_shape = [jax.ShapeDtypeStruct((16, 2 * B), jnp.float32)]
    out_specs = [VMEM]
    bank = (GROUP, 2 * TILE, 2 * TILE)
    if again:
        operands.append(kept)
        specs.append(pl.BlockSpec(memory_space=pl.ANY))
    else:
        out_shape.append(jax.ShapeDtypeStruct((KEPT[own],) + bank, jnp.bfloat16))
        out_specs.append(pl.BlockSpec(memory_space=pl.ANY))
    if bases:
        out_shape.append(jax.ShapeDtypeStruct((256, TILE), jnp.float32))
        out_specs.append(VMEM)
    return pl.pallas_call(
        partial(apply_kernel, own, again),
        out_shape=out_shape,
        in_specs=specs,
        out_specs=out_specs,
        scratch_shapes=[
            pltpu.VMEM((slots, 8, TILE), jnp.float32),
            pltpu.VMEM((slots, 8, TILE), jnp.float32),
            pltpu.VMEM((slots, 32, TILE), jnp.bfloat16),
            pltpu.VMEM((slots, 32, TILE), jnp.bfloat16),
            pltpu.VMEM((3 * GROUP, TILE, TILE), jnp.float32),
            pltpu.VMEM((KEPT[own] + 1,) + bank, jnp.bfloat16),
            pltpu.VMEM((GROUP, 32, 2 * TILE), jnp.bfloat16),
            pltpu.VMEM((rows, 32, TILE), jnp.float32),
            pltpu.VMEM((rows, TILE), jnp.int32),
            pltpu.SMEM((rows, TILE), jnp.int32),
            pltpu.SemaphoreType.DMA,
            pltpu.SemaphoreType.DMA((KEPT[own],)),
        ],
        compiler_params=PARAMS,
        name=("again_" if again else "apply_") + ("own" if own else "cross"),
    )(*operands)


def shards(right_side, points, active):
    column = lax.axis_index("blk")
    member = lax.axis_index("rep")
    sides = right_side.shape[0] // lax.axis_size("rep")
    place = jnp.stack([column, member]).astype(jnp.int32)

    def neighbours(values):
        return from_behind(values, "blk", 1), from_behind(values, "blk", -1)

    rows, cols, rank, box = sort_points(place, points, right_side)
    around = neighbours(rows)
    fixed = (place, active, cols, box)
    part, kept_own = apply_pairs(fixed, (rows,), (rows,))
    w0, kept_cross = apply_pairs(fixed, around, around, part)
    w0_around = neighbours(w0)
    w0_all = lax.all_gather(unsort(w0, rank), "rep", axis=0, tiled=True)
    (part,) = apply_pairs(fixed, (rows,), (w0,), kept=kept_own)
    w1, line = apply_pairs(fixed, around, w0_around, part, (rows, w0), kept_cross)
    line, mine = lax.optimization_barrier((line, unsort(w1, rank)))
    w1_all = lax.all_gather(mine, "rep", axis=0, tiled=True)
    lines = lax.all_to_all(line[:, 0:64], ("blk", "rep"), 0, 0, tiled=True)
    members = lax.axis_size("rep")
    sums = jnp.sum(lines.reshape(-1, members, 4, sides), axis=0)
    sums = jnp.transpose(sums, (1, 0, 2)).reshape(4, members * sides)
    s00, s01, s11, s12 = (sums[k] for k in range(4))
    image_norm = shift * s00 + s01
    alpha = s00 / image_norm
    keep = s01 / image_norm
    rr1 = alpha * alpha * (s11 - s01 * (s01 / s00))
    beta = rr1 / s00
    both = keep + beta
    curved = both * both * s01 - 2.0 * both * alpha * s11 + alpha * alpha * s12
    alpha1 = rr1 / (shift * rr1 * (1.0 + beta) + curved)
    factors = jnp.stack(
        [
            (s00 + s01) / image_norm - noise_level * alpha1 * both,
            noise_level * alpha1 * alpha,
            keep - shift * alpha1 * both,
            shift * alpha1 * alpha - alpha - alpha1 * both,
            alpha1 * alpha,
        ]
    )
    factor = factors[:, :, None]
    posterior = factor[0] * right_side + factor[1] * w0_all
    residual = factor[2] * right_side + factor[3] * w0_all + factor[4] * w1_all
    return (posterior, residual)


def solution(mesh):
    return jax.shard_map(
        shards,
        mesh=mesh,
        in_specs=(P(None, "blk"), P(None, "blk"), P()),
        out_specs=(P(None, "blk"), P(None, "blk")),
        check_vma=False,
    )
```

```python
from functools import partial

import jax
import jax.numpy as jnp
from jax import lax
from jax.experimental import pallas as pl
from jax.experimental.pallas import tpu as pltpu
from jax.sharding import PartitionSpec as P

B = 2048
SUB = 64
TILE = 128
STRIP = 256
BATCH = 4
GROUP = 4
KEPT = {True: 24, False: 8}
EARLY = {True: 12, False: 4}
CELLS_X = 4
CELLS_Y = 8
CELLS = CELLS_X * CELLS_Y
FAR = 1.0e6

support_radius = 2.5
noise_level = 8.0
shift = noise_level + 1.0
profile_scale = 4.0 / support_radius**5
VMEM = pl.BlockSpec(memory_space=pltpu.VMEM)
SMEM = pl.BlockSpec(memory_space=pltpu.SMEM)
ANY = pl.BlockSpec(memory_space=pl.ANY)
LIMIT = 48 * 1024 * 1024


def from_behind(block, axis, distance):
    devices = range(lax.axis_size(axis))
    route = [(i - distance, i) for i in devices if i - distance in devices]
    return lax.ppermute(block, axis, route)


def exchange(values, mask, axis):
    devices = range(lax.axis_size(axis))
    return lax.ppermute(values, axis, [(i, i ^ mask) for i in devices])


def split3(values):
    high = values.astype(jnp.bfloat16)
    rest = values - high.astype(jnp.float32)
    middle = rest.astype(jnp.bfloat16)
    low = (rest - middle.astype(jnp.float32)).astype(jnp.bfloat16)
    return high, middle, low


def one_hot_strip(rank, start):
    place = lax.broadcasted_iota(jnp.int32, (STRIP, B), 0) + start
    return jnp.where(rank == place, 1.0, 0.0).astype(jnp.bfloat16)


def cell_of(values, cells):
    low = jnp.min(values, axis=1, keepdims=True)
    high = jnp.max(values, axis=1, keepdims=True)
    scaled = (values - low) * (cells / jnp.maximum(high - low, 1e-30))
    return jnp.minimum(jnp.floor(scaled), cells - 1.0)


def sort_kernel(
    count,
    meta_ref,
    points_hbm,
    sides_ref,
    rows_ref,
    cols_ref,
    rank_ref,
    box_ref,
    vector_ref,
    feature_ref,
    split_ref,
    edge_ref,
    points_ref,
    arrived,
):
    first = pl.multiple_of(meta_ref[1] * 16, 16)
    locate = pltpu.make_async_copy(points_hbm, points_ref, arrived.at[0])
    locate.start()
    fetch = pltpu.make_async_copy(
        sides_ref.at[pl.ds(first, 16), :], vector_ref, arrived.at[1]
    )
    fetch.start()
    for own in (True, False):
        box_ref[2 if own else 3] = pair_flags(own, meta_ref, count, box_ref.shape[1:])
    upper = lax.broadcasted_iota(jnp.int32, (TILE, TILE), 0) <= lax.broadcasted_iota(
        jnp.int32, (TILE, TILE), 1
    )
    upper = jnp.where(upper, 1.0, 0.0).astype(jnp.bfloat16)
    lower = lax.broadcasted_iota(jnp.int32, (CELLS, CELLS), 0) > lax.broadcasted_iota(
        jnp.int32, (CELLS, CELLS), 1
    )
    lower = jnp.where(lower, 1.0, 0.0)
    number = lax.broadcasted_iota(jnp.int32, (CELLS, TILE), 0).astype(jnp.float32)
    feature_ref[16:32, :] = jnp.zeros((16, B), jnp.float32)
    split_ref[96:128, :] = jnp.zeros((32, B), jnp.bfloat16)
    locate.wait()
    for c in range(2):
        span = slice(c * B, (c + 1) * B)
        cell = cell_of(points_ref[0:1, span], CELLS_X) * CELLS_Y + cell_of(
            points_ref[1:2, span], CELLS_Y
        )
        base = jnp.zeros((CELLS, TILE), jnp.float32)
        chosen, place = [], []
        for t in range(B // TILE):
            hit = jnp.where(number == cell[:, t * TILE : (t + 1) * TILE], 1.0, 0.0)
            count = jnp.dot(hit.astype(jnp.bfloat16), upper, preferred_element_type=jnp.float32)
            chosen.append(hit)
            place.append(count + base)
            base = base + count[:, TILE - 1 :]
        offset = jnp.dot(
            lower, base, precision=lax.Precision.HIGHEST, preferred_element_type=jnp.float32
        )
        for t in range(B // TILE):
            rank = jnp.sum(chosen[t] * (place[t] + (offset - 1.0)), axis=0, keepdims=True)
            rank_ref[0:1, c * B + t * TILE : c * B + (t + 1) * TILE] = rank.astype(jnp.int32)
        if c == 0:
            fetch.wait()
        feature_ref[0:16, :] = vector_ref[:, span]
        feature_ref[16:19, :] = points_ref[:, span]
        for k, part in enumerate(split3(feature_ref[...])):
            split_ref[32 * k : 32 * k + 32, :] = part
        rank = rank_ref[0:1, span]
        for k in range(B // STRIP):
            found = lax.dot_general(
                one_hot_strip(rank, k * STRIP),
                split_ref[...],
                (((1,), (1,)), ((), ())),
                preferred_element_type=jnp.float32,
            )
            found = found + pltpu.roll(found, 96, 1) + pltpu.roll(found, 64, 1)
            spot = slice(c * B + k * STRIP, c * B + (k + 1) * STRIP)
            cols_ref[spot, :] = found
            rows_ref[:, spot] = found.T[0:24, :]
            for t in range(STRIP // SUB):
                chunk = c * (B // SUB) + k * (STRIP // SUB) + t
                piece = found[t * SUB : (t + 1) * SUB, :]
                for e, edge in enumerate((jnp.min, jnp.max)):
                    value = edge(piece, axis=0, keepdims=True)
                    edge_ref[e, chunk : chunk + 1, :] = value
                    edge_ref[e, 64 + chunk : 65 + chunk, :] = value
            for t in range(STRIP // TILE):
                j = c * (B // TILE) + k * (STRIP // TILE) + t
                piece = found[t * TILE : (t + 1) * TILE, :]
                for e, edge in enumerate((jnp.min, jnp.max)):
                    box_ref[e, j : j + 1, :] = edge(piece, axis=0, keepdims=True)
    for e in range(2):
        turned = edge_ref[e].T
        for axis in range(3):
            rows_ref[19 + e : 20 + e, axis * TILE : (axis + 1) * TILE] = turned[
                16 + axis : 17 + axis, :
            ]


def sort_points(count, meta, points, right_side):
    width = 2 * B
    return pl.pallas_call(
        partial(sort_kernel, count),
        out_shape=(
            jax.ShapeDtypeStruct((24, width), jnp.float32),
            jax.ShapeDtypeStruct((width, TILE), jnp.float32),
            jax.ShapeDtypeStruct((8, width), jnp.int32),
            jax.ShapeDtypeStruct((4, width // TILE, TILE), jnp.float32),
        ),
        in_specs=[SMEM, ANY, ANY],
        out_specs=(VMEM, VMEM, VMEM, VMEM),
        scratch_shapes=[
            pltpu.VMEM((16, width), jnp.float32),
            pltpu.VMEM((32, B), jnp.float32),
            pltpu.VMEM((128, B), jnp.bfloat16),
            pltpu.VMEM((2, TILE, TILE), jnp.float32),
            pltpu.VMEM((3, width), jnp.float32),
            pltpu.SemaphoreType.DMA((2,)),
        ],
        compiler_params=pltpu.CompilerParams(vmem_limit_bytes=LIMIT),
        name="sort_points",
    )(meta, points, right_side)


def unsort_kernel(sorted_ref, rank_ref, out_ref, split_ref, total_ref):
    for c in range(2):
        span = slice(c * B, (c + 1) * B)
        for k, part in enumerate(split3(sorted_ref[:, span])):
            split_ref[16 * k : 16 * k + 16, :] = part
        rank = rank_ref[0:1, span]
        for k in range(B // STRIP):
            found = jnp.dot(
                split_ref[:, k * STRIP : (k + 1) * STRIP],
                one_hot_strip(rank, k * STRIP),
                preferred_element_type=jnp.float32,
            )
            total_ref[...] = found if k == 0 else total_ref[...] + found
        out_ref[:, span] = (total_ref[0:16, :] + total_ref[16:32, :]) + total_ref[32:48, :]


def unsort(values, rank):
    return pl.pallas_call(
        unsort_kernel,
        out_shape=jax.ShapeDtypeStruct(values.shape, jnp.float32),
        in_specs=[VMEM, VMEM],
        out_specs=VMEM,
        scratch_shapes=[pltpu.VMEM((48, B), jnp.bfloat16), pltpu.VMEM((48, B), jnp.float32)],
        compiler_params=pltpu.CompilerParams(vmem_limit_bytes=LIMIT),
        name="unsort",
    )(values, rank)


def pair_flags(own, meta_ref, count, shape):
    is_second = lax.broadcasted_iota(jnp.int32, shape, 0) >= shape[0] // 2
    quarter = lax.broadcasted_iota(jnp.int32, shape, 1) // (TILE // 4)
    column = meta_ref[0]
    if own:
        flag = jnp.where(is_second == (quarter == 1), 1, meta_ref[2])
        return jnp.where(quarter < 2, flag, 0).astype(jnp.float32)
    has_behind = jnp.where(column >= 1, 1, 0)
    has_ahead = jnp.where(column + 1 < count, 1, 0)
    flag = jnp.zeros(shape, jnp.int32)
    for c in range(2):
        for q in range(4):
            if q < 2:
                value = meta_ref[8 + 2 * q + c] * has_behind
            else:
                value = meta_ref[3 + 2 * c + (q - 2)] * has_ahead
            flag = jnp.where((is_second == (c == 1)) & (quarter == q), value, flag)
    return flag.astype(jnp.float32)


def pair_table(own, box_ref, xyz_refs, null):
    shape = box_ref.shape[1:]
    lane = lax.broadcasted_iota(jnp.int32, shape, 1)
    total = jnp.zeros(shape, jnp.float32)
    for axis in range(3):
        low_t = box_ref[0, :, 16 + axis : 17 + axis]
        high_t = box_ref[1, :, 16 + axis : 17 + axis]
        span = slice(axis * TILE, (axis + 1) * TILE)
        edges = [[ref[19 + e : 20 + e, span] for e in range(2)] for ref in xyz_refs]
        if own:
            low_s, high_s = edges[0]
        else:
            is_before = lane[0:1] < SUB
            low_s, high_s = (jnp.where(is_before, edges[0][e], edges[1][e]) for e in range(2))
        gap = jnp.maximum(jnp.maximum(low_s - high_t, low_t - high_s), 0.0)
        total = total + gap * gap
    near = total <= support_radius * support_radius * (1.0 + 1e-4)
    near = near & (box_ref[2 if own else 3] > 0.0)
    upper = lax.broadcasted_iota(jnp.int32, (TILE, TILE), 0) <= lax.broadcasted_iota(
        jnp.int32, (TILE, TILE), 1
    )
    place = jnp.dot(
        jnp.where(near, 1.0, 0.0).astype(jnp.bfloat16),
        jnp.where(upper, 1.0, 0.0).astype(jnp.bfloat16),
        preferred_element_type=jnp.float32,
    ).astype(jnp.int32)
    value = jnp.where(near, lane, null)
    left = jnp.where(near, lane + 1 - place, 0)
    for bit in range(7):
        amount = 1 << bit
        next_value = pltpu.roll(value, TILE - amount, 1)
        next_left = pltpu.roll(left, TILE - amount, 1)
        arrives = (next_left & amount) > 0
        stays = (left & amount) == 0
        value = jnp.where(arrives, next_value, jnp.where(stays, value, null))
        left = jnp.where(arrives, next_left, jnp.where(stays, left, 0))
    return value + 256 * place[:, TILE - 1 :]


def apply_kernel(own, again, *refs):
    refs = list(refs)
    cols_ref, box_ref = refs[:2]
    del refs[:2]
    sources = 1 if own else 2
    xyz_refs = [refs.pop(0) for _ in range(sources)]
    vec_refs = [refs.pop(0) for _ in range(sources)]
    add_ref = None if own else refs.pop(0)
    sums = again and not own
    base_refs = [refs.pop(0) for _ in range(2)] if sums else None
    if again:
        list_ref, kept_ref = refs.pop(0), refs.pop(0)
    out_ref = refs.pop(0)
    if not again:
        table_ref, kept_ref = refs.pop(0), refs.pop(0)
    sums_ref = refs.pop(0) if sums else None
    left_xyz, right_xyz, left_w, right_w, target, bank, weights, total_ref, moved = refs[:9]
    rows = out_ref.shape[1] // TILE
    cells = rows // GROUP
    kept = KEPT[own]
    null = 2 * rows * sources
    lane = lax.broadcasted_iota(jnp.int32, (8, TILE), 1)
    is_left = lane < SUB

    def transfer(g):
        ends = (kept_ref.at[g], bank.at[g]) if again else (bank.at[g], kept_ref.at[g])
        return pltpu.make_async_copy(*ends, moved.at[g])

    if again:
        for g in range(EARLY[own]):
            transfer(g).start()
    else:
        list_ref, arrived = refs[9:]
        table_ref[...] = pair_table(own, box_ref, xyz_refs, null)
        load = pltpu.make_async_copy(table_ref, list_ref, arrived)
        load.start()

    def spread(values):
        turned = pltpu.roll(values, SUB, 1)
        mask = jnp.concatenate([is_left] * (values.shape[0] // 8), axis=0)
        zero = jnp.zeros_like(values)
        return (
            jnp.where(mask, values, zero),
            jnp.where(mask, zero, turned),
            jnp.where(mask, turned, zero),
            jnp.where(mask, zero, values),
        )

    def parts(values):
        high = values.astype(jnp.bfloat16)
        low = (values - high.astype(jnp.float32)).astype(jnp.bfloat16)
        return jnp.concatenate([high, low], axis=0)

    def prepare_xyz(s, spot, slot):
        xyz = spread(xyz_refs[s][16:24, spot])
        left_xyz[slot] = xyz[0]
        right_xyz[slot] = xyz[1]
        left_xyz[slot + 1] = xyz[2]
        right_xyz[slot + 1] = xyz[3]

    for s in range(sources):

        def prepare(g, carry):
            for u in range(4):
                t = g * 4 + u
                spot = pl.ds(pl.multiple_of(t * TILE, TILE), TILE)
                slot = 2 * (t + s * rows)
                if not again:
                    prepare_xyz(s, spot, slot)
                vec = spread(vec_refs[s][0:16, spot])
                left_w[slot] = parts(vec[0])
                right_w[slot] = parts(vec[1])
                left_w[slot + 1] = parts(vec[2])
                right_w[slot + 1] = parts(vec[3])
            return carry

        lax.fori_loop(0, rows // 4, prepare, 0)
    left_xyz[null] = jnp.where(is_left, FAR, 0.0)
    right_xyz[null] = jnp.where(is_left, 0.0, FAR)
    left_w[null] = jnp.zeros((32, TILE), jnp.bfloat16)
    right_w[null] = jnp.zeros((32, TILE), jnp.bfloat16)
    total_ref[...] = jnp.zeros_like(total_ref)
    bank[kept] = jnp.zeros(bank.shape[1:], jnp.bfloat16)
    weights[...] = jnp.zeros_like(weights)

    def members(cell):
        mirror = cell + 3 * cells // 2 - cells * (cell // (cells // 2))
        return cell, mirror, rows - 1 - mirror, rows - 1 - cell

    def batches(cell):
        count = list_ref[cell, 0]
        for j in members(cell)[1:]:
            count = jnp.maximum(count, list_ref[j, 0])
        return (count // 256 + BATCH - 1) // BATCH

    def aim(cell):
        for k, j in enumerate(members(cell)):
            spot = pl.ds(pl.multiple_of(j * TILE, TILE), TILE)
            for axis in range(3):
                target[3 * k + axis] = jnp.broadcast_to(
                    cols_ref[spot, 16 + axis : 17 + axis], (TILE, TILE)
                )

    def chunks(j, n, s):
        return list_ref[j, 4 * n + 2 * s] & 255, list_ref[j, 4 * n + 2 * s + 1] & 255

    def weigh(k, j, n):
        for s in range(2):
            first, second = chunks(j, n, s)
            weights[k, :, s * TILE : (s + 1) * TILE] = left_w[first] + right_w[second]

    def form(slot, k, j, n):
        for s in range(2):
            first, second = chunks(j, n, s)
            xyz = left_xyz[first] + right_xyz[second]
            here = slice(s * TILE, (s + 1) * TILE)
            for r in range(TILE // 16):
                span = slice(16 * r, 16 * r + 16)
                dx = target[3 * k, span, :] - xyz[0:1, :]
                dy = target[3 * k + 1, span, :] - xyz[1:2, :]
                dz = target[3 * k + 2, span, :] - xyz[2:3, :]
                square = jnp.maximum(dx * dx + dy * dy + dz * dz, 1e-30)
                distance = square * lax.rsqrt(square)
                inside = jnp.maximum(support_radius - distance, 0.0)
                inside = inside * inside
                value = (inside * inside) * (distance + 0.25 * support_radius)
                high = value.astype(jnp.bfloat16)
                low = (value - high.astype(jnp.float32)).astype(jnp.bfloat16)
                bank[slot, k, 16 * r : 16 * r + 16, here] = high
                bank[slot, k, TILE + 16 * r : TILE + 16 * r + 16, here] = low

    def apply(slot, k):
        both = lax.dot_general(
            weights[k],
            bank[slot, k],
            (((1,), (1,)), ((), ())),
            preferred_element_type=jnp.float32,
        )
        return both[:, 0:TILE] + both[:, TILE : 2 * TILE]

    def add(cell, images):
        for j, image in zip(members(cell), images):
            total_ref[j] += image

    if not again:
        load.wait()
    needed = lax.fori_loop(0, cells, lambda cell, n: n + batches(cell), 0)
    used = jnp.minimum(needed, kept)

    if again:
        early = EARLY[own]
        lax.fori_loop(early, used, lambda g, carry: (transfer(g).start(), carry)[1], 0)

        @pl.when(needed > kept)
        def _():
            for s in range(sources):

                def prepare_again(t, carry):
                    spot = pl.ds(pl.multiple_of(t * TILE, TILE), TILE)
                    prepare_xyz(s, spot, 2 * (t + s * rows))
                    return carry

                lax.fori_loop(0, rows, prepare_again, 0)

        def row_group(cell, g):
            def step(n, g):
                slot = jnp.minimum(g, kept)

                @pl.when(g < kept)
                def _():
                    transfer(g).wait()

                @pl.when(g >= kept)
                def _():
                    aim(cell)
                    for k, j in enumerate(members(cell)):
                        form(slot, k, j, n)

                for k, j in enumerate(members(cell)):
                    weigh(k, j, n)
                add(cell, [apply(slot, k) for k in range(GROUP)])
                return g + 1

            return lax.fori_loop(0, batches(cell), step, g)

        lax.fori_loop(0, cells, row_group, 0)
        lax.fori_loop(used, early, lambda g, carry: (transfer(g).wait(), carry)[1], 0)
    else:

        def row_group(cell, state):
            count = batches(cell)

            @pl.when(count > 0)
            def _():
                aim(cell)

            def step(n, state):
                g, last_slot, last_cell = state
                slot = jnp.minimum(g, kept)
                images = [apply(last_slot, k) for k in range(GROUP)]
                for k, j in enumerate(members(cell)):
                    weigh(k, j, n)
                    form(slot, k, j, n)
                add(last_cell, images)

                @pl.when(g < kept)
                def _():
                    transfer(g).start()

                return g + 1, slot, cell

            return lax.fori_loop(0, count, step, state)

        _, slot, cell = lax.fori_loop(0, cells, row_group, (0, kept, 0))
        add(cell, [apply(slot, k) for k in range(GROUP)])

    def finish(g, running):
        for u in range(4):
            j = g * 4 + u
            spot = pl.ds(pl.multiple_of(j * TILE, TILE), TILE)
            total = total_ref[j]
            image = (total[0:16, :] + total[16:32, :]) * profile_scale
            if own:
                held = (left_w[2 * j] + right_w[2 * j + 1]).astype(jnp.float32)
                image = image - (held[0:16, :] + held[16:32, :])
            else:
                image = image + add_ref[:, spot]
            out_ref[:, spot] = image
            if sums:
                side = base_refs[0][0:16, spot]
                first = base_refs[1][:, spot]
                running = (
                    running[0] + side * side,
                    running[1] + side * first,
                    running[2] + first * first,
                    running[3] + first * image,
                )
        return running

    zero = jnp.zeros((16, TILE), jnp.float32)
    result = lax.fori_loop(0, rows // 4, finish, (zero,) * 4 if sums else 0)
    if not again:
        lax.fori_loop(0, used, lambda g, carry: (transfer(g).wait(), carry)[1], 0)
    if sums:
        columns = lax.broadcasted_iota(jnp.int32, (16, TILE), 1)
        packed = zero
        for k in range(4):
            packed = jnp.where(columns == k, jnp.sum(result[k], axis=1, keepdims=True), packed)
        turned = jnp.concatenate([packed] + [zero] * 7, axis=0).T
        line = turned[0:1]
        for k in range(1, 4):
            line = line + pltpu.roll(turned[k : k + 1], 16 * k, 1)
        sums_ref[...] = jnp.broadcast_to(line, sums_ref.shape)


def apply_pairs(fixed, coords, vectors, added=None, bases=(), kept=None):
    own = added is None
    again = kept is not None
    operands = [*fixed, *coords, *vectors]
    operands += ([] if own else [added]) + list(bases)
    specs = [VMEM] * len(operands)
    rows = 2 * B // TILE
    slots = 2 * rows * len(coords) + 1
    out_shape = [jax.ShapeDtypeStruct((16, 2 * B), jnp.float32)]
    out_specs = [VMEM]
    bank = (GROUP, 2 * TILE, 2 * TILE)
    if again:
        operands += kept
        specs += [SMEM, ANY]
        scratch = []
    else:
        out_shape.append(jax.ShapeDtypeStruct((rows, TILE), jnp.int32))
        out_shape.append(jax.ShapeDtypeStruct((KEPT[own],) + bank, jnp.bfloat16))
        out_specs += [VMEM, ANY]
        scratch = [pltpu.SMEM((rows, TILE), jnp.int32), pltpu.SemaphoreType.DMA]
    if bases:
        out_shape.append(jax.ShapeDtypeStruct((256, TILE), jnp.float32))
        out_specs.append(VMEM)
    return pl.pallas_call(
        partial(apply_kernel, own, again),
        out_shape=out_shape,
        in_specs=specs,
        out_specs=out_specs,
        scratch_shapes=[
            pltpu.VMEM((slots, 8, TILE), jnp.float32),
            pltpu.VMEM((slots, 8, TILE), jnp.float32),
            pltpu.VMEM((slots, 32, TILE), jnp.bfloat16),
            pltpu.VMEM((slots, 32, TILE), jnp.bfloat16),
            pltpu.VMEM((3 * GROUP, TILE, TILE), jnp.float32),
            pltpu.VMEM((KEPT[own] + 1,) + bank, jnp.bfloat16),
            pltpu.VMEM((GROUP, 32, 2 * TILE), jnp.bfloat16),
            pltpu.VMEM((rows, 32, TILE), jnp.float32),
            pltpu.SemaphoreType.DMA((KEPT[own],)),
            *scratch,
        ],
        compiler_params=pltpu.CompilerParams(vmem_limit_bytes=LIMIT),
        name=("again_" if again else "apply_") + ("own" if own else "cross"),
    )(*operands)


def finish_kernel(lines_ref, sides_ref, w0_ref, *refs):
    pieces, (posterior_ref, residual_ref, factor_ref) = refs[:4], refs[4:]

    @pl.when(pl.program_id(0) == 0)
    def _():
        lines = lines_ref[...]
        row = lax.broadcasted_iota(jnp.int32, lines.shape, 0)
        sums = [
            jnp.sum(jnp.where((row & 3) == q, lines, 0.0), axis=0, keepdims=True)
            for q in range(4)
        ]
        sums = jnp.concatenate(sums + [jnp.zeros((4, lines.shape[1]), jnp.float32)], axis=0)
        sums = jnp.concatenate([sums, jnp.ones_like(sums)], axis=1)
        sums = jnp.concatenate([sums, jnp.ones((TILE - 8, TILE), jnp.float32)], axis=0).T
        s00, s01, s11, s12 = (sums[16 * k : 16 * k + 16] for k in range(4))
        image_norm = shift * s00 + s01
        alpha = s00 / image_norm
        keep = s01 / image_norm
        rr1 = alpha * alpha * (s11 - s01 * (s01 / s00))
        beta = rr1 / s00
        both = keep + beta
        curved = both * both * s01 - 2.0 * both * alpha * s11 + alpha * alpha * s12
        alpha1 = rr1 / (shift * rr1 * (1.0 + beta) + curved)
        factor_ref[0] = (s00 + s01) / image_norm - noise_level * alpha1 * both
        factor_ref[1] = noise_level * alpha1 * alpha
        factor_ref[2] = keep - shift * alpha1 * both
        factor_ref[3] = shift * alpha1 * alpha - alpha - alpha1 * both
        factor_ref[4] = alpha1 * alpha

    for member in range(4):

        @pl.when(lax.axis_index("rep") == member)
        def _():
            for q in range(4):
                rows = slice(16 * q, 16 * q + 16)
                factor = [factor_ref[k, :, q : q + 1] for k in range(5)]
                side = sides_ref[rows, :]
                first = w0_ref[rows, :]
                second = pieces[q ^ member][...]
                posterior_ref[rows, :] = factor[0] * side + factor[1] * first
                residual_ref[rows, :] = (
                    factor[2] * side + factor[3] * first + factor[4] * second
                )


def finish_sides(lines, right_side, w0_all, pieces):
    width = 1024
    full = pl.BlockSpec((64, width), lambda i: (0, i))
    part = pl.BlockSpec((16, width), lambda i: (0, i))
    shape = jax.ShapeDtypeStruct(right_side.shape, jnp.float32)
    return pl.pallas_call(
        finish_kernel,
        grid=(right_side.shape[1] // width,),
        out_shape=(shape, shape),
        in_specs=[pl.BlockSpec(lines.shape, lambda i: (0, 0)), full, full] + [part] * 4,
        out_specs=(full, full),
        scratch_shapes=[pltpu.VMEM((5, 16, TILE), jnp.float32)],
        compiler_params=pltpu.CompilerParams(vmem_limit_bytes=LIMIT),
        name="finish_sides",
    )(lines, right_side, w0_all, *pieces)


def shards(right_side, points, active):
    column = lax.axis_index("blk")
    member = lax.axis_index("rep")
    sides = right_side.shape[0] // lax.axis_size("rep")
    here = lax.dynamic_slice_in_dim(active, column, 1, 0)[0]
    before = lax.dynamic_slice_in_dim(active, jnp.maximum(column - 1, 0), 1, 0)[0]
    place = jnp.stack([column, member]).astype(jnp.int32)
    meta = jnp.concatenate([place, here, before])

    def neighbours(values):
        return from_behind(values, "blk", 1), from_behind(values, "blk", -1)

    rows, cols, rank, box = sort_points(lax.axis_size("blk"), meta, points, right_side)
    around = neighbours(rows)
    fixed = (cols, box)
    part, *kept_own = apply_pairs(fixed, (rows,), (rows,))
    w0, *kept_cross = apply_pairs(fixed, around, around, part)
    w0_around = neighbours(w0)
    w0_all = lax.all_gather(unsort(w0, rank), "rep", axis=0, tiled=True)
    (part,) = apply_pairs(fixed, (rows,), (w0,), kept=kept_own)
    w1, line = apply_pairs(fixed, around, w0_around, part, (rows, w0), kept_cross)
    line, mine = lax.optimization_barrier((line, unsort(w1, rank)))
    pieces = [mine] + [exchange(mine, mask, "rep") for mask in (1, 3, 2)]
    pieces = [pieces[k] for k in (0, 1, 3, 2)]
    lines = lax.all_to_all(line[:, 0:64], ("blk", "rep"), 0, 0, tiled=True)
    return finish_sides(lines, right_side, w0_all, pieces)


def solution(mesh):
    return jax.shard_map(
        shards,
        mesh=mesh,
        in_specs=(P(None, "blk"), P(None, "blk"), P()),
        out_specs=(P(None, "blk"), P(None, "blk")),
        check_vma=False,
    )
```

```python
from functools import partial

import jax
import jax.numpy as jnp
from jax import lax
from jax.experimental import pallas as pl
from jax.experimental.pallas import tpu as pltpu
from jax.sharding import PartitionSpec as P

B = 2048
SUB = 64
TILE = 128
STRIP = 256
BATCH = 4
GROUP = 4
KEPT = {True: 24, False: 8}
EARLY = {True: 12, False: 4}
CELLS_X = 4
CELLS_Y = 8
CELLS = CELLS_X * CELLS_Y
FAR = 1.0e6

support_radius = 2.5
noise_level = 8.0
shift = noise_level + 1.0
profile_scale = 4.0 / support_radius**5
VMEM = pl.BlockSpec(memory_space=pltpu.VMEM)
SMEM = pl.BlockSpec(memory_space=pltpu.SMEM)
ANY = pl.BlockSpec(memory_space=pl.ANY)
LIMIT = 48 * 1024 * 1024


def from_behind(block, axis, distance):
    devices = range(lax.axis_size(axis))
    route = [(i - distance, i) for i in devices if i - distance in devices]
    return lax.ppermute(block, axis, route)


def exchange(values, mask, axis):
    devices = range(lax.axis_size(axis))
    return lax.ppermute(values, axis, [(i, i ^ mask) for i in devices])


def split3(values):
    high = values.astype(jnp.bfloat16)
    rest = values - high.astype(jnp.float32)
    middle = rest.astype(jnp.bfloat16)
    low = (rest - middle.astype(jnp.float32)).astype(jnp.bfloat16)
    return high, middle, low


def one_hot_strip(rank, start):
    place = lax.broadcasted_iota(jnp.int32, (STRIP, B), 0) + start
    return jnp.where(rank == place, 1.0, 0.0).astype(jnp.bfloat16)


def cell_of(values, cells):
    low = jnp.min(values, axis=1, keepdims=True)
    high = jnp.max(values, axis=1, keepdims=True)
    scaled = (values - low) * (cells / jnp.maximum(high - low, 1e-30))
    return jnp.minimum(jnp.floor(scaled), cells - 1.0)


def sort_kernel(
    count,
    meta_ref,
    points_hbm,
    sides_ref,
    rows_ref,
    cols_ref,
    rank_ref,
    box_ref,
    vector_ref,
    feature_ref,
    split_ref,
    edge_ref,
    points_ref,
    arrived,
):
    first = pl.multiple_of(meta_ref[1] * 16, 16)
    locate = pltpu.make_async_copy(points_hbm, points_ref, arrived.at[0])
    locate.start()
    fetch = pltpu.make_async_copy(
        sides_ref.at[pl.ds(first, 16), :], vector_ref, arrived.at[1]
    )
    fetch.start()
    for own in (True, False):
        box_ref[2 if own else 3] = pair_flags(own, meta_ref, count, box_ref.shape[1:])
    upper = lax.broadcasted_iota(jnp.int32, (TILE, TILE), 0) <= lax.broadcasted_iota(
        jnp.int32, (TILE, TILE), 1
    )
    upper = jnp.where(upper, 1.0, 0.0).astype(jnp.bfloat16)
    lower = lax.broadcasted_iota(jnp.int32, (CELLS, CELLS), 0) > lax.broadcasted_iota(
        jnp.int32, (CELLS, CELLS), 1
    )
    lower = jnp.where(lower, 1.0, 0.0)
    number = lax.broadcasted_iota(jnp.int32, (CELLS, TILE), 0).astype(jnp.float32)
    feature_ref[16:32, :] = jnp.zeros((16, B), jnp.float32)
    split_ref[96:128, :] = jnp.zeros((32, B), jnp.bfloat16)
    locate.wait()
    for c in range(2):
        span = slice(c * B, (c + 1) * B)
        cell = cell_of(points_ref[0:1, span], CELLS_X) * CELLS_Y + cell_of(
            points_ref[1:2, span], CELLS_Y
        )
        base = jnp.zeros((CELLS, TILE), jnp.float32)
        chosen, place = [], []
        for t in range(B // TILE):
            hit = jnp.where(number == cell[:, t * TILE : (t + 1) * TILE], 1.0, 0.0)
            count = jnp.dot(hit.astype(jnp.bfloat16), upper, preferred_element_type=jnp.float32)
            chosen.append(hit)
            place.append(count + base)
            base = base + count[:, TILE - 1 :]
        offset = jnp.dot(
            lower, base, precision=lax.Precision.HIGHEST, preferred_element_type=jnp.float32
        )
        for t in range(B // TILE):
            rank = jnp.sum(chosen[t] * (place[t] + (offset - 1.0)), axis=0, keepdims=True)
            rank_ref[0:1, c * B + t * TILE : c * B + (t + 1) * TILE] = rank.astype(jnp.int32)
        if c == 0:
            fetch.wait()
        feature_ref[0:16, :] = vector_ref[:, span]
        feature_ref[16:19, :] = points_ref[:, span]
        for k, part in enumerate(split3(feature_ref[...])):
            split_ref[32 * k : 32 * k + 32, :] = part
        rank = rank_ref[0:1, span]
        for k in range(B // STRIP):
            found = lax.dot_general(
                one_hot_strip(rank, k * STRIP),
                split_ref[...],
                (((1,), (1,)), ((), ())),
                preferred_element_type=jnp.float32,
            )
            found = found + pltpu.roll(found, 96, 1) + pltpu.roll(found, 64, 1)
            spot = slice(c * B + k * STRIP, c * B + (k + 1) * STRIP)
            cols_ref[spot, :] = found
            rows_ref[:, spot] = found.T[0:24, :]
            for t in range(STRIP // SUB):
                chunk = c * (B // SUB) + k * (STRIP // SUB) + t
                piece = found[t * SUB : (t + 1) * SUB, :]
                for e, edge in enumerate((jnp.min, jnp.max)):
                    value = edge(piece, axis=0, keepdims=True)
                    edge_ref[e, chunk : chunk + 1, :] = value
                    edge_ref[e, 64 + chunk : 65 + chunk, :] = value
            for t in range(STRIP // TILE):
                j = c * (B // TILE) + k * (STRIP // TILE) + t
                piece = found[t * TILE : (t + 1) * TILE, :]
                for e, edge in enumerate((jnp.min, jnp.max)):
                    box_ref[e, j : j + 1, :] = edge(piece, axis=0, keepdims=True)
    for e in range(2):
        turned = edge_ref[e].T
        for axis in range(3):
            rows_ref[19 + e : 20 + e, axis * TILE : (axis + 1) * TILE] = turned[
                16 + axis : 17 + axis, :
            ]


def sort_points(count, meta, points, right_side):
    width = 2 * B
    return pl.pallas_call(
        partial(sort_kernel, count),
        out_shape=(
            jax.ShapeDtypeStruct((24, width), jnp.float32),
            jax.ShapeDtypeStruct((width, TILE), jnp.float32),
            jax.ShapeDtypeStruct((8, width), jnp.int32),
            jax.ShapeDtypeStruct((4, width // TILE, TILE), jnp.float32),
        ),
        in_specs=[SMEM, ANY, ANY],
        out_specs=(VMEM, VMEM, VMEM, VMEM),
        scratch_shapes=[
            pltpu.VMEM((16, width), jnp.float32),
            pltpu.VMEM((32, B), jnp.float32),
            pltpu.VMEM((128, B), jnp.bfloat16),
            pltpu.VMEM((2, TILE, TILE), jnp.float32),
            pltpu.VMEM((3, width), jnp.float32),
            pltpu.SemaphoreType.DMA((2,)),
        ],
        compiler_params=pltpu.CompilerParams(vmem_limit_bytes=LIMIT),
        name="sort_points",
    )(meta, points, right_side)


def unsort_kernel(sorted_ref, rank_ref, out_ref, split_ref, total_ref):
    for c in range(2):
        span = slice(c * B, (c + 1) * B)
        for k, part in enumerate(split3(sorted_ref[:, span])):
            split_ref[16 * k : 16 * k + 16, :] = part
        rank = rank_ref[0:1, span]
        for k in range(B // STRIP):
            found = jnp.dot(
                split_ref[:, k * STRIP : (k + 1) * STRIP],
                one_hot_strip(rank, k * STRIP),
                preferred_element_type=jnp.float32,
            )
            total_ref[...] = found if k == 0 else total_ref[...] + found
        out_ref[:, span] = (total_ref[0:16, :] + total_ref[16:32, :]) + total_ref[32:48, :]


def unsort(values, rank):
    return pl.pallas_call(
        unsort_kernel,
        out_shape=jax.ShapeDtypeStruct(values.shape, jnp.float32),
        in_specs=[VMEM, VMEM],
        out_specs=VMEM,
        scratch_shapes=[pltpu.VMEM((48, B), jnp.bfloat16), pltpu.VMEM((48, B), jnp.float32)],
        compiler_params=pltpu.CompilerParams(vmem_limit_bytes=LIMIT),
        name="unsort",
    )(values, rank)


def pair_flags(own, meta_ref, count, shape):
    is_second = lax.broadcasted_iota(jnp.int32, shape, 0) >= shape[0] // 2
    quarter = lax.broadcasted_iota(jnp.int32, shape, 1) // (TILE // 4)
    column = meta_ref[0]
    if own:
        flag = jnp.where(is_second == (quarter == 1), 1, meta_ref[2])
        return jnp.where(quarter < 2, flag, 0).astype(jnp.float32)
    has_behind = jnp.where(column >= 1, 1, 0)
    has_ahead = jnp.where(column + 1 < count, 1, 0)
    flag = jnp.zeros(shape, jnp.int32)
    for c in range(2):
        for q in range(4):
            if q < 2:
                value = meta_ref[8 + 2 * q + c] * has_behind
            else:
                value = meta_ref[3 + 2 * c + (q - 2)] * has_ahead
            flag = jnp.where((is_second == (c == 1)) & (quarter == q), value, flag)
    return flag.astype(jnp.float32)


def pair_table(own, box_ref, xyz_refs, null):
    shape = box_ref.shape[1:]
    lane = lax.broadcasted_iota(jnp.int32, shape, 1)
    total = jnp.zeros(shape, jnp.float32)
    for axis in range(3):
        low_t = box_ref[0, :, 16 + axis : 17 + axis]
        high_t = box_ref[1, :, 16 + axis : 17 + axis]
        span = slice(axis * TILE, (axis + 1) * TILE)
        edges = [[ref[19 + e : 20 + e, span] for e in range(2)] for ref in xyz_refs]
        if own:
            low_s, high_s = edges[0]
        else:
            is_before = lane[0:1] < SUB
            low_s, high_s = (jnp.where(is_before, edges[0][e], edges[1][e]) for e in range(2))
        gap = jnp.maximum(jnp.maximum(low_s - high_t, low_t - high_s), 0.0)
        total = total + gap * gap
    near = total <= support_radius * support_radius * (1.0 + 1e-4)
    near = near & (box_ref[2 if own else 3] > 0.0)
    upper = lax.broadcasted_iota(jnp.int32, (TILE, TILE), 0) <= lax.broadcasted_iota(
        jnp.int32, (TILE, TILE), 1
    )
    place = jnp.dot(
        jnp.where(near, 1.0, 0.0).astype(jnp.bfloat16),
        jnp.where(upper, 1.0, 0.0).astype(jnp.bfloat16),
        preferred_element_type=jnp.float32,
    ).astype(jnp.int32)
    value = jnp.where(near, lane, null)
    left = jnp.where(near, lane + 1 - place, 0)
    for bit in range(7):
        amount = 1 << bit
        next_value = pltpu.roll(value, TILE - amount, 1)
        next_left = pltpu.roll(left, TILE - amount, 1)
        arrives = (next_left & amount) > 0
        stays = (left & amount) == 0
        value = jnp.where(arrives, next_value, jnp.where(stays, value, null))
        left = jnp.where(arrives, next_left, jnp.where(stays, left, 0))
    return value + 256 * place[:, TILE - 1 :]


def apply_kernel(own, again, *refs):
    refs = list(refs)
    cols_ref, box_ref = refs[:2]
    del refs[:2]
    sources = 1 if own else 2
    xyz_refs = [refs.pop(0) for _ in range(sources)]
    vec_refs = [refs.pop(0) for _ in range(sources)]
    add_ref = None if own else refs.pop(0)
    sums = again and not own
    base_refs = [refs.pop(0) for _ in range(2)] if sums else None
    if again:
        list_ref, kept_ref = refs.pop(0), refs.pop(0)
    out_ref = refs.pop(0)
    if not again:
        table_ref, kept_ref = refs.pop(0), refs.pop(0)
    sums_ref = refs.pop(0) if sums else None
    left_xyz, right_xyz, left_w, right_w, target, bank, weights, total_ref, moved = refs[:9]
    rows = out_ref.shape[1] // TILE
    cells = rows // GROUP
    kept = KEPT[own]
    null = 2 * rows * sources
    lane = lax.broadcasted_iota(jnp.int32, (8, TILE), 1)
    is_left = lane < SUB

    def transfer(g):
        ends = (kept_ref.at[g], bank.at[g]) if again else (bank.at[g], kept_ref.at[g])
        return pltpu.make_async_copy(*ends, moved.at[g])

    if again:
        for g in range(EARLY[own]):
            transfer(g).start()
    else:
        list_ref, arrived = refs[9:]
        table_ref[...] = pair_table(own, box_ref, xyz_refs, null)
        load = pltpu.make_async_copy(table_ref, list_ref, arrived)
        load.start()

    def spread(values):
        turned = pltpu.roll(values, SUB, 1)
        mask = jnp.concatenate([is_left] * (values.shape[0] // 8), axis=0)
        zero = jnp.zeros_like(values)
        return (
            jnp.where(mask, values, zero),
            jnp.where(mask, zero, turned),
            jnp.where(mask, turned, zero),
            jnp.where(mask, zero, values),
        )

    def parts(values):
        high = values.astype(jnp.bfloat16)
        low = (values - high.astype(jnp.float32)).astype(jnp.bfloat16)
        return jnp.concatenate([high, low], axis=0)

    def prepare_xyz(s, spot, slot):
        xyz = spread(xyz_refs[s][16:24, spot])
        left_xyz[slot] = xyz[0]
        right_xyz[slot] = xyz[1]
        left_xyz[slot + 1] = xyz[2]
        right_xyz[slot + 1] = xyz[3]

    for s in range(sources):

        def prepare(g, carry):
            for u in range(4):
                t = g * 4 + u
                spot = pl.ds(pl.multiple_of(t * TILE, TILE), TILE)
                slot = 2 * (t + s * rows)
                if not again:
                    prepare_xyz(s, spot, slot)
                vec = spread(vec_refs[s][0:16, spot])
                left_w[slot] = parts(vec[0])
                right_w[slot] = parts(vec[1])
                left_w[slot + 1] = parts(vec[2])
                right_w[slot + 1] = parts(vec[3])
            return carry

        lax.fori_loop(0, rows // 4, prepare, 0)
    left_xyz[null] = jnp.where(is_left, FAR, 0.0)
    right_xyz[null] = jnp.where(is_left, 0.0, FAR)
    left_w[null] = jnp.zeros((32, TILE), jnp.bfloat16)
    right_w[null] = jnp.zeros((32, TILE), jnp.bfloat16)
    total_ref[...] = jnp.zeros_like(total_ref)
    bank[kept] = jnp.zeros(bank.shape[1:], jnp.bfloat16)
    weights[...] = jnp.zeros_like(weights)

    def members(cell):
        mirror = cell + 3 * cells // 2 - cells * (cell // (cells // 2))
        return cell, mirror, rows - 1 - mirror, rows - 1 - cell

    def batches(cell):
        count = list_ref[cell, 0]
        for j in members(cell)[1:]:
            count = jnp.maximum(count, list_ref[j, 0])
        return (count // 256 + BATCH - 1) // BATCH

    def aim(cell):
        for k, j in enumerate(members(cell)):
            spot = pl.ds(pl.multiple_of(j * TILE, TILE), TILE)
            for axis in range(3):
                target[3 * k + axis] = jnp.broadcast_to(
                    cols_ref[spot, 16 + axis : 17 + axis], (TILE, TILE)
                )

    def chunks(j, n, s):
        return list_ref[j, 4 * n + 2 * s] & 255, list_ref[j, 4 * n + 2 * s + 1] & 255

    def weigh(k, j, n):
        for s in range(2):
            first, second = chunks(j, n, s)
            weights[k, :, s * TILE : (s + 1) * TILE] = left_w[first] + right_w[second]

    def form(slot, k, j, n):
        for s in range(2):
            first, second = chunks(j, n, s)
            xyz = left_xyz[first] + right_xyz[second]
            here = slice(s * TILE, (s + 1) * TILE)
            for r in range(TILE // 16):
                span = slice(16 * r, 16 * r + 16)
                dx = target[3 * k, span, :] - xyz[0:1, :]
                dy = target[3 * k + 1, span, :] - xyz[1:2, :]
                dz = target[3 * k + 2, span, :] - xyz[2:3, :]
                square = jnp.maximum(dx * dx + dy * dy + dz * dz, 1e-30)
                distance = square * lax.rsqrt(square)
                inside = jnp.maximum(support_radius - distance, 0.0)
                inside = inside * inside
                value = (inside * inside) * (distance + 0.25 * support_radius)
                high = value.astype(jnp.bfloat16)
                low = (value - high.astype(jnp.float32)).astype(jnp.bfloat16)
                bank[slot, k, 16 * r : 16 * r + 16, here] = high
                bank[slot, k, TILE + 16 * r : TILE + 16 * r + 16, here] = low

    def apply(slot, k):
        both = lax.dot_general(
            weights[k],
            bank[slot, k],
            (((1,), (1,)), ((), ())),
            preferred_element_type=jnp.float32,
        )
        return both[:, 0:TILE] + both[:, TILE : 2 * TILE]

    def add(cell, images):
        for j, image in zip(members(cell), images):
            total_ref[j] += image

    if not again:
        load.wait()
    needed = lax.fori_loop(0, cells, lambda cell, n: n + batches(cell), 0)
    used = jnp.minimum(needed, kept)

    if again:
        early = EARLY[own]
        lax.fori_loop(early, used, lambda g, carry: (transfer(g).start(), carry)[1], 0)

        @pl.when(needed > kept)
        def _():
            for s in range(sources):

                def prepare_again(t, carry):
                    spot = pl.ds(pl.multiple_of(t * TILE, TILE), TILE)
                    prepare_xyz(s, spot, 2 * (t + s * rows))
                    return carry

                lax.fori_loop(0, rows, prepare_again, 0)

        def row_group(cell, g):
            def step(n, g):
                slot = jnp.minimum(g, kept)

                @pl.when(g < kept)
                def _():
                    transfer(g).wait()

                @pl.when(g >= kept)
                def _():
                    aim(cell)
                    for k, j in enumerate(members(cell)):
                        form(slot, k, j, n)

                for k, j in enumerate(members(cell)):
                    weigh(k, j, n)
                add(cell, [apply(slot, k) for k in range(GROUP)])
                return g + 1

            return lax.fori_loop(0, batches(cell), step, g)

        lax.fori_loop(0, cells, row_group, 0)
        lax.fori_loop(used, early, lambda g, carry: (transfer(g).wait(), carry)[1], 0)
    else:

        def row_group(cell, state):
            count = batches(cell)

            @pl.when(count > 0)
            def _():
                aim(cell)

            def step(n, state):
                g, last_slot, last_cell = state
                slot = jnp.minimum(g, kept)
                images = [apply(last_slot, k) for k in range(GROUP)]
                for k, j in enumerate(members(cell)):
                    weigh(k, j, n)
                    form(slot, k, j, n)
                add(last_cell, images)

                @pl.when(g < kept)
                def _():
                    transfer(g).start()

                return g + 1, slot, cell

            return lax.fori_loop(0, count, step, state)

        _, slot, cell = lax.fori_loop(0, cells, row_group, (0, kept, 0))
        add(cell, [apply(slot, k) for k in range(GROUP)])

    def finish(g, running):
        for u in range(4):
            j = g * 4 + u
            spot = pl.ds(pl.multiple_of(j * TILE, TILE), TILE)
            total = total_ref[j]
            image = (total[0:16, :] + total[16:32, :]) * profile_scale
            if own:
                held = (left_w[2 * j] + right_w[2 * j + 1]).astype(jnp.float32)
                image = image - (held[0:16, :] + held[16:32, :])
            else:
                image = image + add_ref[:, spot]
            out_ref[:, spot] = image
            if sums:
                side = base_refs[0][0:16, spot]
                first = base_refs[1][:, spot]
                running = (
                    running[0] + side * side,
                    running[1] + side * first,
                    running[2] + first * first,
                    running[3] + first * image,
                )
        return running

    zero = jnp.zeros((16, TILE), jnp.float32)
    result = lax.fori_loop(0, rows // 4, finish, (zero,) * 4 if sums else 0)
    if not again:
        lax.fori_loop(0, used, lambda g, carry: (transfer(g).wait(), carry)[1], 0)
    if sums:
        columns = lax.broadcasted_iota(jnp.int32, (16, TILE), 1)
        packed = zero
        for k in range(4):
            packed = jnp.where(columns == k, jnp.sum(result[k], axis=1, keepdims=True), packed)
        turned = jnp.concatenate([packed] + [zero] * 7, axis=0).T
        line = turned[0:1]
        for k in range(1, 4):
            line = line + pltpu.roll(turned[k : k + 1], 16 * k, 1)
        sums_ref[...] = jnp.broadcast_to(line, sums_ref.shape)


def apply_pairs(fixed, coords, vectors, added=None, bases=(), kept=None):
    own = added is None
    again = kept is not None
    operands = [*fixed, *coords, *vectors]
    operands += ([] if own else [added]) + list(bases)
    specs = [VMEM] * len(operands)
    rows = 2 * B // TILE
    slots = 2 * rows * len(coords) + 1
    out_shape = [jax.ShapeDtypeStruct((16, 2 * B), jnp.float32)]
    out_specs = [VMEM]
    bank = (GROUP, 2 * TILE, 2 * TILE)
    if again:
        operands += kept
        specs += [SMEM, ANY]
        scratch = []
    else:
        out_shape.append(jax.ShapeDtypeStruct((rows, TILE), jnp.int32))
        out_shape.append(jax.ShapeDtypeStruct((KEPT[own],) + bank, jnp.bfloat16))
        out_specs += [VMEM, ANY]
        scratch = [pltpu.SMEM((rows, TILE), jnp.int32), pltpu.SemaphoreType.DMA]
    if bases:
        out_shape.append(jax.ShapeDtypeStruct((256, TILE), jnp.float32))
        out_specs.append(VMEM)
    return pl.pallas_call(
        partial(apply_kernel, own, again),
        out_shape=out_shape,
        in_specs=specs,
        out_specs=out_specs,
        scratch_shapes=[
            pltpu.VMEM((slots, 8, TILE), jnp.float32),
            pltpu.VMEM((slots, 8, TILE), jnp.float32),
            pltpu.VMEM((slots, 32, TILE), jnp.bfloat16),
            pltpu.VMEM((slots, 32, TILE), jnp.bfloat16),
            pltpu.VMEM((3 * GROUP, TILE, TILE), jnp.float32),
            pltpu.VMEM((KEPT[own] + 1,) + bank, jnp.bfloat16),
            pltpu.VMEM((GROUP, 32, 2 * TILE), jnp.bfloat16),
            pltpu.VMEM((rows, 32, TILE), jnp.float32),
            pltpu.SemaphoreType.DMA((KEPT[own],)),
            *scratch,
        ],
        compiler_params=pltpu.CompilerParams(vmem_limit_bytes=LIMIT),
        name=("again_" if again else "apply_") + ("own" if own else "cross"),
    )(*operands)


def finish_kernel(lines_ref, sides_ref, *refs):
    posterior_ref, residual_ref, factor_ref = refs[8:]

    @pl.when(pl.program_id(0) == 0)
    def _():
        lines = lines_ref[...]
        row = lax.broadcasted_iota(jnp.int32, lines.shape, 0)
        sums = [
            jnp.sum(jnp.where((row & 3) == q, lines, 0.0), axis=0, keepdims=True)
            for q in range(4)
        ]
        sums = jnp.concatenate(sums + [jnp.zeros((4, lines.shape[1]), jnp.float32)], axis=0)
        sums = jnp.concatenate([sums, jnp.ones_like(sums)], axis=1)
        sums = jnp.concatenate([sums, jnp.ones((TILE - 8, TILE), jnp.float32)], axis=0).T
        s00, s01, s11, s12 = (sums[16 * k : 16 * k + 16] for k in range(4))
        image_norm = shift * s00 + s01
        alpha = s00 / image_norm
        keep = s01 / image_norm
        rr1 = alpha * alpha * (s11 - s01 * (s01 / s00))
        beta = rr1 / s00
        both = keep + beta
        curved = both * both * s01 - 2.0 * both * alpha * s11 + alpha * alpha * s12
        alpha1 = rr1 / (shift * rr1 * (1.0 + beta) + curved)
        factor_ref[0] = (s00 + s01) / image_norm - noise_level * alpha1 * both
        factor_ref[1] = noise_level * alpha1 * alpha
        factor_ref[2] = keep - shift * alpha1 * both
        factor_ref[3] = shift * alpha1 * alpha - alpha - alpha1 * both
        factor_ref[4] = alpha1 * alpha

    for member in range(4):

        @pl.when(lax.axis_index("rep") == member)
        def _():
            for q in range(4):
                rows = slice(16 * q, 16 * q + 16)
                factor = [factor_ref[k, :, q : q + 1] for k in range(5)]
                side = sides_ref[rows, :]
                first = refs[q ^ member][...]
                second = refs[4 + (q ^ member)][...]
                posterior_ref[rows, :] = factor[0] * side + factor[1] * first
                residual_ref[rows, :] = (
                    factor[2] * side + factor[3] * first + factor[4] * second
                )


def finish_sides(lines, right_side, pieces):
    width = 1024
    full = pl.BlockSpec((64, width), lambda i: (0, i))
    part = pl.BlockSpec((16, width), lambda i: (0, i))
    shape = jax.ShapeDtypeStruct(right_side.shape, jnp.float32)
    return pl.pallas_call(
        finish_kernel,
        grid=(right_side.shape[1] // width,),
        out_shape=(shape, shape),
        in_specs=[pl.BlockSpec(lines.shape, lambda i: (0, 0)), full] + [part] * 8,
        out_specs=(full, full),
        scratch_shapes=[pltpu.VMEM((5, 16, TILE), jnp.float32)],
        compiler_params=pltpu.CompilerParams(vmem_limit_bytes=LIMIT),
        name="finish_sides",
    )(lines, right_side, *pieces)


def shards(right_side, points, active):
    column = lax.axis_index("blk")
    member = lax.axis_index("rep")
    sides = right_side.shape[0] // lax.axis_size("rep")
    here = lax.dynamic_slice_in_dim(active, column, 1, 0)[0]
    before = lax.dynamic_slice_in_dim(active, jnp.maximum(column - 1, 0), 1, 0)[0]
    place = jnp.stack([column, member]).astype(jnp.int32)
    meta = jnp.concatenate([place, here, before])

    def spread(values):
        return [values] + [exchange(values, mask, "rep") for mask in (1, 2, 3)]

    def neighbours(values):
        return from_behind(values, "blk", 1), from_behind(values, "blk", -1)

    rows, cols, rank, box = sort_points(lax.axis_size("blk"), meta, points, right_side)
    around = neighbours(rows)
    fixed = (cols, box)
    part, *kept_own = apply_pairs(fixed, (rows,), (rows,))
    w0, *kept_cross = apply_pairs(fixed, around, around, part)
    w0_around = neighbours(w0)
    w0_pieces = spread(unsort(w0, rank))
    (part,) = apply_pairs(fixed, (rows,), (w0,), kept=kept_own)
    w1, line = apply_pairs(fixed, around, w0_around, part, (rows, w0), kept_cross)
    line, mine = lax.optimization_barrier((line, unsort(w1, rank)))
    w1_pieces = spread(mine)
    lines = lax.all_to_all(line[:, 0:64], ("blk", "rep"), 0, 0, tiled=True)
    return finish_sides(lines, right_side, w0_pieces + w1_pieces)


def solution(mesh):
    return jax.shard_map(
        shards,
        mesh=mesh,
        in_specs=(P(None, "blk"), P(None, "blk"), P()),
        out_specs=(P(None, "blk"), P(None, "blk")),
        check_vma=False,
    )
```

```python
from functools import partial

import jax
import jax.numpy as jnp
from jax import lax
from jax.experimental import pallas as pl
from jax.experimental.pallas import tpu as pltpu
from jax.sharding import PartitionSpec as P

B = 2048
SUB = 64
TILE = 128
STRIP = 256
BATCH = 4
GROUP = 4
KEPT = {True: 24, False: 8}
EARLY = {True: 12, False: 4}
CELLS_X = 4
CELLS_Y = 8
CELLS = CELLS_X * CELLS_Y
FAR = 1.0e6

support_radius = 2.5
noise_level = 8.0
shift = noise_level + 1.0
profile_scale = 4.0 / support_radius**5
VMEM = pl.BlockSpec(memory_space=pltpu.VMEM)
SMEM = pl.BlockSpec(memory_space=pltpu.SMEM)
ANY = pl.BlockSpec(memory_space=pl.ANY)
LIMIT = 48 * 1024 * 1024


def from_behind(block, axis, distance):
    devices = range(lax.axis_size(axis))
    route = [(i - distance, i) for i in devices if i - distance in devices]
    return lax.ppermute(block, axis, route)


def exchange(values, mask, axis):
    devices = range(lax.axis_size(axis))
    return lax.ppermute(values, axis, [(i, i ^ mask) for i in devices])


def split3(values):
    high = values.astype(jnp.bfloat16)
    rest = values - high.astype(jnp.float32)
    middle = rest.astype(jnp.bfloat16)
    low = (rest - middle.astype(jnp.float32)).astype(jnp.bfloat16)
    return high, middle, low


def one_hot_strip(rank, start):
    place = lax.broadcasted_iota(jnp.int32, (TILE, B), 0).astype(jnp.bfloat16)
    one, zero = jnp.ones((), jnp.bfloat16), jnp.zeros((), jnp.bfloat16)
    blocks = []
    for t in range(STRIP // TILE):
        local = rank - (start + t * TILE)
        local = jnp.where((local >= 0) & (local < TILE), local, -1)
        local = local.astype(jnp.float32).astype(jnp.bfloat16)
        blocks.append(jnp.where(local == place, one, zero))
    return jnp.concatenate(blocks, axis=0)


def cell_of(values, cells):
    low = jnp.min(values, axis=1, keepdims=True)
    high = jnp.max(values, axis=1, keepdims=True)
    scaled = (values - low) * (cells / jnp.maximum(high - low, 1e-30))
    return jnp.minimum(jnp.floor(scaled), cells - 1.0)


def sort_kernel(
    count,
    active_ref,
    points_hbm,
    sides_ref,
    rows_ref,
    cols_ref,
    rank_ref,
    box_ref,
    vector_ref,
    feature_ref,
    split_ref,
    edge_ref,
    points_ref,
    arrived,
):
    column = lax.axis_index("blk")
    first = pl.multiple_of(lax.axis_index("rep") * 16, 16)
    locate = pltpu.make_async_copy(points_hbm, points_ref, arrived.at[0])
    locate.start()
    fetch = pltpu.make_async_copy(
        sides_ref.at[pl.ds(first, 16), :], vector_ref, arrived.at[1]
    )
    fetch.start()
    for own in (True, False):
        box_ref[2 if own else 3] = pair_flags(own, active_ref, column, count, box_ref.shape[1:])
    upper = lax.broadcasted_iota(jnp.int32, (TILE, TILE), 0) <= lax.broadcasted_iota(
        jnp.int32, (TILE, TILE), 1
    )
    upper = jnp.where(upper, 1.0, 0.0).astype(jnp.bfloat16)
    lower = lax.broadcasted_iota(jnp.int32, (CELLS, CELLS), 0) > lax.broadcasted_iota(
        jnp.int32, (CELLS, CELLS), 1
    )
    lower = jnp.where(lower, 1.0, 0.0).astype(jnp.bfloat16)
    number = lax.broadcasted_iota(jnp.int32, (CELLS, TILE), 0).astype(jnp.float32)
    feature_ref[16:32, :] = jnp.zeros((16, B), jnp.float32)
    split_ref[96:128, :] = jnp.zeros((32, B), jnp.bfloat16)
    locate.wait()
    for c in range(2):
        span = slice(c * B, (c + 1) * B)
        cell = cell_of(points_ref[0:1, span], CELLS_X) * CELLS_Y + cell_of(
            points_ref[1:2, span], CELLS_Y
        )
        base = jnp.zeros((CELLS, TILE), jnp.float32)
        chosen = [
            jnp.where(number == cell[:, t * TILE : (t + 1) * TILE], 1.0, 0.0)
            for t in range(B // TILE)
        ]
        counts = jnp.dot(
            jnp.concatenate(chosen, axis=0).astype(jnp.bfloat16),
            upper,
            preferred_element_type=jnp.float32,
        )
        place = []
        for t in range(B // TILE):
            count = counts[t * CELLS : (t + 1) * CELLS, :]
            place.append(count + base)
            base = base + count[:, TILE - 1 :]
        high = jnp.floor(base * (1.0 / 64.0))
        offset = jnp.dot(
            lower,
            jnp.concatenate([high, base - 64.0 * high], axis=1).astype(jnp.bfloat16),
            preferred_element_type=jnp.float32,
        )
        offset = 64.0 * offset[:, 0:TILE] + offset[:, TILE : 2 * TILE]
        for t in range(B // TILE):
            rank = jnp.sum(chosen[t] * (place[t] + (offset - 1.0)), axis=0, keepdims=True)
            rank_ref[0:1, c * B + t * TILE : c * B + (t + 1) * TILE] = rank.astype(jnp.int32)
        if c == 0:
            fetch.wait()
        feature_ref[0:16, :] = vector_ref[:, span]
        feature_ref[16:19, :] = points_ref[:, span]
        for k, part in enumerate(split3(feature_ref[...])):
            split_ref[32 * k : 32 * k + 32, :] = part
        rank = rank_ref[0:1, span]
        for k in range(B // STRIP):
            found = lax.dot_general(
                one_hot_strip(rank, k * STRIP),
                split_ref[...],
                (((1,), (1,)), ((), ())),
                preferred_element_type=jnp.float32,
            )
            found = found + pltpu.roll(found, 96, 1) + pltpu.roll(found, 64, 1)
            spot = slice(c * B + k * STRIP, c * B + (k + 1) * STRIP)
            cols_ref[spot, :] = found
            rows_ref[:, spot] = found.T[0:24, :]
            for t in range(STRIP // SUB):
                chunk = c * (B // SUB) + k * (STRIP // SUB) + t
                piece = found[t * SUB : (t + 1) * SUB, :]
                for e, edge in enumerate((jnp.min, jnp.max)):
                    value = edge(piece, axis=0, keepdims=True)
                    edge_ref[e, chunk : chunk + 1, :] = value
                    edge_ref[e, 64 + chunk : 65 + chunk, :] = value
            for t in range(STRIP // TILE):
                j = c * (B // TILE) + k * (STRIP // TILE) + t
                piece = found[t * TILE : (t + 1) * TILE, :]
                for e, edge in enumerate((jnp.min, jnp.max)):
                    box_ref[e, j : j + 1, :] = edge(piece, axis=0, keepdims=True)
    for e in range(2):
        turned = edge_ref[e].T
        for axis in range(3):
            rows_ref[19 + e : 20 + e, axis * TILE : (axis + 1) * TILE] = turned[
                16 + axis : 17 + axis, :
            ]


def sort_points(count, active, points, right_side):
    width = 2 * B
    return pl.pallas_call(
        partial(sort_kernel, count),
        out_shape=(
            jax.ShapeDtypeStruct((24, width), jnp.float32),
            jax.ShapeDtypeStruct((width, TILE), jnp.float32),
            jax.ShapeDtypeStruct((8, width), jnp.int32),
            jax.ShapeDtypeStruct((4, width // TILE, TILE), jnp.float32),
        ),
        in_specs=[SMEM, ANY, ANY],
        out_specs=(VMEM, VMEM, VMEM, VMEM),
        scratch_shapes=[
            pltpu.VMEM((16, width), jnp.float32),
            pltpu.VMEM((32, B), jnp.float32),
            pltpu.VMEM((128, B), jnp.bfloat16),
            pltpu.VMEM((2, TILE, TILE), jnp.float32),
            pltpu.VMEM((3, width), jnp.float32),
            pltpu.SemaphoreType.DMA((2,)),
        ],
        compiler_params=pltpu.CompilerParams(vmem_limit_bytes=LIMIT),
        name="sort_points",
    )(active, points, right_side)


def unsort_kernel(sorted_ref, rank_ref, out_ref, split_ref, total_ref):
    for c in range(2):
        span = slice(c * B, (c + 1) * B)
        for k, part in enumerate(split3(sorted_ref[:, span])):
            split_ref[16 * k : 16 * k + 16, :] = part
        rank = rank_ref[0:1, span]
        for k in range(B // STRIP):
            found = jnp.dot(
                split_ref[:, k * STRIP : (k + 1) * STRIP],
                one_hot_strip(rank, k * STRIP),
                preferred_element_type=jnp.float32,
            )
            total_ref[...] = found if k == 0 else total_ref[...] + found
        out_ref[:, span] = (total_ref[0:16, :] + total_ref[16:32, :]) + total_ref[32:48, :]


def unsort(values, rank):
    return pl.pallas_call(
        unsort_kernel,
        out_shape=jax.ShapeDtypeStruct(values.shape, jnp.float32),
        in_specs=[VMEM, VMEM],
        out_specs=VMEM,
        scratch_shapes=[pltpu.VMEM((48, B), jnp.bfloat16), pltpu.VMEM((48, B), jnp.float32)],
        compiler_params=pltpu.CompilerParams(vmem_limit_bytes=LIMIT),
        name="unsort",
    )(values, rank)


def pair_flags(own, active_ref, column, count, shape):
    is_second = lax.broadcasted_iota(jnp.int32, shape, 0) >= shape[0] // 2
    quarter = lax.broadcasted_iota(jnp.int32, shape, 1) // (TILE // 4)
    if own:
        flag = jnp.where(is_second == (quarter == 1), 1, active_ref[0, column])
        return jnp.where(quarter < 2, flag, 0).astype(jnp.float32)
    behind = jnp.maximum(column - 1, 0)
    has_behind = jnp.where(column >= 1, 1, 0)
    has_ahead = jnp.where(column + 1 < count, 1, 0)
    flag = jnp.zeros(shape, jnp.int32)
    for c in range(2):
        for q in range(4):
            if q < 2:
                value = active_ref[1 + 2 * q + c, behind] * has_behind
            else:
                value = active_ref[1 + 2 * c + (q - 2), column] * has_ahead
            flag = jnp.where((is_second == (c == 1)) & (quarter == q), value, flag)
    return flag.astype(jnp.float32)


def pair_table(own, box_ref, xyz_refs, null):
    shape = box_ref.shape[1:]
    lane = lax.broadcasted_iota(jnp.int32, shape, 1)
    total = jnp.zeros(shape, jnp.float32)
    for axis in range(3):
        low_t = box_ref[0, :, 16 + axis : 17 + axis]
        high_t = box_ref[1, :, 16 + axis : 17 + axis]
        span = slice(axis * TILE, (axis + 1) * TILE)
        edges = [[ref[19 + e : 20 + e, span] for e in range(2)] for ref in xyz_refs]
        if own:
            low_s, high_s = edges[0]
        else:
            is_before = lane[0:1] < SUB
            low_s, high_s = (jnp.where(is_before, edges[0][e], edges[1][e]) for e in range(2))
        gap = jnp.maximum(jnp.maximum(low_s - high_t, low_t - high_s), 0.0)
        total = total + gap * gap
    near = total <= support_radius * support_radius * (1.0 + 1e-4)
    near = near & (box_ref[2 if own else 3] > 0.0)
    upper = lax.broadcasted_iota(jnp.int32, (TILE, TILE), 0) <= lax.broadcasted_iota(
        jnp.int32, (TILE, TILE), 1
    )
    place = jnp.dot(
        jnp.where(near, 1.0, 0.0).astype(jnp.bfloat16),
        jnp.where(upper, 1.0, 0.0).astype(jnp.bfloat16),
        preferred_element_type=jnp.float32,
    ).astype(jnp.int32)
    value = jnp.where(near, lane, null)
    left = jnp.where(near, lane + 1 - place, 0)
    for bit in range(7):
        amount = 1 << bit
        next_value = pltpu.roll(value, TILE - amount, 1)
        next_left = pltpu.roll(left, TILE - amount, 1)
        arrives = (next_left & amount) > 0
        stays = (left & amount) == 0
        value = jnp.where(arrives, next_value, jnp.where(stays, value, null))
        left = jnp.where(arrives, next_left, jnp.where(stays, left, 0))
    return value + 256 * place[:, TILE - 1 :]


def apply_kernel(own, again, *refs):
    refs = list(refs)
    cols_ref, box_ref = refs[:2]
    del refs[:2]
    sources = 1 if own else 2
    xyz_refs = [refs.pop(0) for _ in range(sources)]
    vec_refs = [refs.pop(0) for _ in range(sources)]
    add_ref = None if own else refs.pop(0)
    sums = again and not own
    base_refs = [refs.pop(0) for _ in range(2)] if sums else None
    if again:
        list_ref, kept_ref = refs.pop(0), refs.pop(0)
    out_ref = refs.pop(0)
    if not again:
        table_ref, kept_ref = refs.pop(0), refs.pop(0)
    sums_ref = refs.pop(0) if sums else None
    left_xyz, right_xyz, left_w, right_w, target, bank, weights, total_ref, moved = refs[:9]
    rows = out_ref.shape[1] // TILE
    cells = rows // GROUP
    kept = KEPT[own]
    null = 2 * rows * sources
    lane = lax.broadcasted_iota(jnp.int32, (8, TILE), 1)
    is_left = lane < SUB

    def transfer(g):
        ends = (kept_ref.at[g], bank.at[g]) if again else (bank.at[g], kept_ref.at[g])
        return pltpu.make_async_copy(*ends, moved.at[g])

    if again:
        for g in range(EARLY[own]):
            transfer(g).start()
    else:
        list_ref, arrived = refs[9:]
        table_ref[...] = pair_table(own, box_ref, xyz_refs, null)
        load = pltpu.make_async_copy(table_ref, list_ref, arrived)
        load.start()

    def spread(values):
        turned = pltpu.roll(values, SUB, 1)
        mask = jnp.concatenate([is_left] * (values.shape[0] // 8), axis=0)
        zero = jnp.zeros_like(values)
        return (
            jnp.where(mask, values, zero),
            jnp.where(mask, zero, turned),
            jnp.where(mask, turned, zero),
            jnp.where(mask, zero, values),
        )

    def parts(values):
        high = values.astype(jnp.bfloat16)
        low = (values - high.astype(jnp.float32)).astype(jnp.bfloat16)
        return jnp.concatenate([high, low], axis=0)

    def prepare_xyz(s, spot, slot):
        xyz = spread(xyz_refs[s][16:24, spot])
        left_xyz[slot] = xyz[0]
        right_xyz[slot] = xyz[1]
        left_xyz[slot + 1] = xyz[2]
        right_xyz[slot + 1] = xyz[3]

    for s in range(sources):

        def prepare(g, carry):
            for u in range(4):
                t = g * 4 + u
                spot = pl.ds(pl.multiple_of(t * TILE, TILE), TILE)
                slot = 2 * (t + s * rows)
                if not again:
                    prepare_xyz(s, spot, slot)
                vec = spread(vec_refs[s][0:16, spot])
                left_w[slot] = parts(vec[0])
                right_w[slot] = parts(vec[1])
                left_w[slot + 1] = parts(vec[2])
                right_w[slot + 1] = parts(vec[3])
            return carry

        lax.fori_loop(0, rows // 4, prepare, 0)
    left_xyz[null] = jnp.where(is_left, FAR, 0.0)
    right_xyz[null] = jnp.where(is_left, 0.0, FAR)
    left_w[null] = jnp.zeros((32, TILE), jnp.bfloat16)
    right_w[null] = jnp.zeros((32, TILE), jnp.bfloat16)
    total_ref[...] = jnp.zeros_like(total_ref)
    bank[kept] = jnp.zeros(bank.shape[1:], jnp.bfloat16)
    weights[...] = jnp.zeros_like(weights)

    def members(cell):
        mirror = cell + 3 * cells // 2 - cells * (cell // (cells // 2))
        return cell, mirror, rows - 1 - mirror, rows - 1 - cell

    def batches(cell):
        count = list_ref[cell, 0]
        for j in members(cell)[1:]:
            count = jnp.maximum(count, list_ref[j, 0])
        return (count // 256 + BATCH - 1) // BATCH

    def aim(cell):
        for k, j in enumerate(members(cell)):
            spot = pl.ds(pl.multiple_of(j * TILE, TILE), TILE)
            for axis in range(3):
                target[3 * k + axis] = jnp.broadcast_to(
                    cols_ref[spot, 16 + axis : 17 + axis], (TILE, TILE)
                )

    def chunks(j, n, s):
        return list_ref[j, 4 * n + 2 * s] & 255, list_ref[j, 4 * n + 2 * s + 1] & 255

    def weigh(k, j, n):
        for s in range(2):
            first, second = chunks(j, n, s)
            weights[k, :, s * TILE : (s + 1) * TILE] = left_w[first] + right_w[second]

    def form(slot, k, j, n):
        for s in range(2):
            first, second = chunks(j, n, s)
            xyz = left_xyz[first] + right_xyz[second]
            here = slice(s * TILE, (s + 1) * TILE)
            for r in range(TILE // 16):
                span = slice(16 * r, 16 * r + 16)
                dx = target[3 * k, span, :] - xyz[0:1, :]
                dy = target[3 * k + 1, span, :] - xyz[1:2, :]
                dz = target[3 * k + 2, span, :] - xyz[2:3, :]
                square = jnp.maximum(dx * dx + dy * dy + dz * dz, 1e-30)
                distance = square * lax.rsqrt(square)
                inside = jnp.maximum(support_radius - distance, 0.0)
                inside = inside * inside
                value = (inside * inside) * (distance + 0.25 * support_radius)
                high = value.astype(jnp.bfloat16)
                low = (value - high.astype(jnp.float32)).astype(jnp.bfloat16)
                bank[slot, k, 16 * r : 16 * r + 16, here] = high
                bank[slot, k, TILE + 16 * r : TILE + 16 * r + 16, here] = low

    def apply(slot, k):
        both = lax.dot_general(
            weights[k],
            bank[slot, k],
            (((1,), (1,)), ((), ())),
            preferred_element_type=jnp.float32,
        )
        return both[:, 0:TILE] + both[:, TILE : 2 * TILE]

    def add(cell, images):
        for j, image in zip(members(cell), images):
            total_ref[j] += image

    if not again:
        load.wait()
    needed = lax.fori_loop(0, cells, lambda cell, n: n + batches(cell), 0)
    used = jnp.minimum(needed, kept)

    if again:
        early = EARLY[own]
        lax.fori_loop(early, used, lambda g, carry: (transfer(g).start(), carry)[1], 0)

        @pl.when(needed > kept)
        def _():
            for s in range(sources):

                def prepare_again(t, carry):
                    spot = pl.ds(pl.multiple_of(t * TILE, TILE), TILE)
                    prepare_xyz(s, spot, 2 * (t + s * rows))
                    return carry

                lax.fori_loop(0, rows, prepare_again, 0)

        def row_group(cell, g):
            def step(n, g):
                slot = jnp.minimum(g, kept)

                @pl.when(g < kept)
                def _():
                    transfer(g).wait()

                @pl.when(g >= kept)
                def _():
                    aim(cell)
                    for k, j in enumerate(members(cell)):
                        form(slot, k, j, n)

                for k, j in enumerate(members(cell)):
                    weigh(k, j, n)
                add(cell, [apply(slot, k) for k in range(GROUP)])
                return g + 1

            return lax.fori_loop(0, batches(cell), step, g)

        lax.fori_loop(0, cells, row_group, 0)
        lax.fori_loop(used, early, lambda g, carry: (transfer(g).wait(), carry)[1], 0)
    else:

        def row_group(cell, state):
            count = batches(cell)

            @pl.when(count > 0)
            def _():
                aim(cell)

            def step(n, state):
                g, last_slot, last_cell = state
                slot = jnp.minimum(g, kept)
                images = [apply(last_slot, k) for k in range(GROUP)]
                for k, j in enumerate(members(cell)):
                    weigh(k, j, n)
                    form(slot, k, j, n)
                add(last_cell, images)

                @pl.when(g < kept)
                def _():
                    transfer(g).start()

                return g + 1, slot, cell

            return lax.fori_loop(0, count, step, state)

        _, slot, cell = lax.fori_loop(0, cells, row_group, (0, kept, 0))
        add(cell, [apply(slot, k) for k in range(GROUP)])

    def finish(g, running):
        for u in range(4):
            j = g * 4 + u
            spot = pl.ds(pl.multiple_of(j * TILE, TILE), TILE)
            total = total_ref[j]
            image = (total[0:16, :] + total[16:32, :]) * profile_scale
            if own:
                held = (left_w[2 * j] + right_w[2 * j + 1]).astype(jnp.float32)
                image = image - (held[0:16, :] + held[16:32, :])
            else:
                image = image + add_ref[:, spot]
            out_ref[:, spot] = image
            if sums:
                side = base_refs[0][0:16, spot]
                first = base_refs[1][:, spot]
                running = (
                    running[0] + side * side,
                    running[1] + side * first,
                    running[2] + first * first,
                    running[3] + first * image,
                )
        return running

    zero = jnp.zeros((16, TILE), jnp.float32)
    result = lax.fori_loop(0, rows // 4, finish, (zero,) * 4 if sums else 0)
    if not again:
        lax.fori_loop(0, used, lambda g, carry: (transfer(g).wait(), carry)[1], 0)
    if sums:
        columns = lax.broadcasted_iota(jnp.int32, (16, TILE), 1)
        packed = zero
        for k in range(4):
            packed = jnp.where(columns == k, jnp.sum(result[k], axis=1, keepdims=True), packed)
        turned = jnp.concatenate([packed] + [zero] * 7, axis=0).T
        line = turned[0:1]
        for k in range(1, 4):
            line = line + pltpu.roll(turned[k : k + 1], 16 * k, 1)
        sums_ref[...] = jnp.broadcast_to(line, sums_ref.shape)


def apply_pairs(fixed, coords, vectors, added=None, bases=(), kept=None):
    own = added is None
    again = kept is not None
    operands = [*fixed, *coords, *vectors]
    operands += ([] if own else [added]) + list(bases)
    specs = [VMEM] * len(operands)
    rows = 2 * B // TILE
    slots = 2 * rows * len(coords) + 1
    out_shape = [jax.ShapeDtypeStruct((16, 2 * B), jnp.float32)]
    out_specs = [VMEM]
    bank = (GROUP, 2 * TILE, 2 * TILE)
    if again:
        operands += kept
        specs += [SMEM, ANY]
        scratch = []
    else:
        out_shape.append(jax.ShapeDtypeStruct((rows, TILE), jnp.int32))
        out_shape.append(jax.ShapeDtypeStruct((KEPT[own],) + bank, jnp.bfloat16))
        out_specs += [VMEM, ANY]
        scratch = [pltpu.SMEM((rows, TILE), jnp.int32), pltpu.SemaphoreType.DMA]
    if bases:
        out_shape.append(jax.ShapeDtypeStruct((256, TILE), jnp.float32))
        out_specs.append(VMEM)
    return pl.pallas_call(
        partial(apply_kernel, own, again),
        out_shape=out_shape,
        in_specs=specs,
        out_specs=out_specs,
        scratch_shapes=[
            pltpu.VMEM((slots, 8, TILE), jnp.float32),
            pltpu.VMEM((slots, 8, TILE), jnp.float32),
            pltpu.VMEM((slots, 32, TILE), jnp.bfloat16),
            pltpu.VMEM((slots, 32, TILE), jnp.bfloat16),
            pltpu.VMEM((3 * GROUP, TILE, TILE), jnp.float32),
            pltpu.VMEM((KEPT[own] + 1,) + bank, jnp.bfloat16),
            pltpu.VMEM((GROUP, 32, 2 * TILE), jnp.bfloat16),
            pltpu.VMEM((rows, 32, TILE), jnp.float32),
            pltpu.SemaphoreType.DMA((KEPT[own],)),
            *scratch,
        ],
        compiler_params=pltpu.CompilerParams(vmem_limit_bytes=LIMIT),
        name=("again_" if again else "apply_") + ("own" if own else "cross"),
    )(*operands)


def finish_kernel(lines_ref, sides_ref, *refs):
    posterior_ref, residual_ref, factor_ref = refs[8:]

    @pl.when(pl.program_id(0) == 0)
    def _():
        lines = lines_ref[...]
        row = lax.broadcasted_iota(jnp.int32, lines.shape, 0)
        sums = [
            jnp.sum(jnp.where((row & 3) == q, lines, 0.0), axis=0, keepdims=True)
            for q in range(4)
        ]
        sums = jnp.concatenate(sums + [jnp.zeros((4, lines.shape[1]), jnp.float32)], axis=0)
        sums = jnp.concatenate([sums, jnp.ones_like(sums)], axis=1)
        sums = jnp.concatenate([sums, jnp.ones((TILE - 8, TILE), jnp.float32)], axis=0).T
        s00, s01, s11, s12 = (sums[16 * k : 16 * k + 16] for k in range(4))
        image_norm = shift * s00 + s01
        alpha = s00 / image_norm
        keep = s01 / image_norm
        rr1 = alpha * alpha * (s11 - s01 * (s01 / s00))
        beta = rr1 / s00
        both = keep + beta
        curved = both * both * s01 - 2.0 * both * alpha * s11 + alpha * alpha * s12
        alpha1 = rr1 / (shift * rr1 * (1.0 + beta) + curved)
        factor_ref[0] = (s00 + s01) / image_norm - noise_level * alpha1 * both
        factor_ref[1] = noise_level * alpha1 * alpha
        factor_ref[2] = keep - shift * alpha1 * both
        factor_ref[3] = shift * alpha1 * alpha - alpha - alpha1 * both
        factor_ref[4] = alpha1 * alpha

    for member in range(4):

        @pl.when(lax.axis_index("rep") == member)
        def _():
            for q in range(4):
                rows = slice(16 * q, 16 * q + 16)
                factor = [factor_ref[k, :, q : q + 1] for k in range(5)]
                side = sides_ref[rows, :]
                first = refs[q ^ member][...]
                second = refs[4 + (q ^ member)][...]
                posterior_ref[rows, :] = factor[0] * side + factor[1] * first
                residual_ref[rows, :] = (
                    factor[2] * side + factor[3] * first + factor[4] * second
                )


def finish_sides(lines, right_side, pieces):
    width = 1024
    full = pl.BlockSpec((64, width), lambda i: (0, i))
    part = pl.BlockSpec((16, width), lambda i: (0, i))
    shape = jax.ShapeDtypeStruct(right_side.shape, jnp.float32)
    return pl.pallas_call(
        finish_kernel,
        grid=(right_side.shape[1] // width,),
        out_shape=(shape, shape),
        in_specs=[pl.BlockSpec(lines.shape, lambda i: (0, 0)), full] + [part] * 8,
        out_specs=(full, full),
        scratch_shapes=[pltpu.VMEM((5, 16, TILE), jnp.float32)],
        compiler_params=pltpu.CompilerParams(vmem_limit_bytes=LIMIT),
        name="finish_sides",
    )(lines, right_side, *pieces)


def shards(right_side, points, active):
    def spread(values):
        return [values] + [exchange(values, mask, "rep") for mask in (1, 2, 3)]

    def neighbours(values):
        return from_behind(values, "blk", 1), from_behind(values, "blk", -1)

    rows, cols, rank, box = sort_points(lax.axis_size("blk"), active.T, points, right_side)
    around = neighbours(rows)
    fixed = (cols, box)
    part, *kept_own = apply_pairs(fixed, (rows,), (rows,))
    w0, *kept_cross = apply_pairs(fixed, around, around, part)
    w0_around = neighbours(w0)
    w0_pieces = spread(unsort(w0, rank))
    (part,) = apply_pairs(fixed, (rows,), (w0,), kept=kept_own)
    w1, line = apply_pairs(fixed, around, w0_around, part, (rows, w0), kept_cross)
    mine = unsort(w1, rank)
    w1_pieces = spread(mine)
    lines = lax.all_to_all(line[:, 0:64], ("blk", "rep"), 0, 0, tiled=True)
    return finish_sides(lines, right_side, w0_pieces + w1_pieces)


def solution(mesh):
    return jax.shard_map(
        shards,
        mesh=mesh,
        in_specs=(P(None, "blk"), P(None, "blk"), P()),
        out_specs=(P(None, "blk"), P(None, "blk")),
        check_vma=False,
    )
```

```python
from functools import partial

import jax
import jax.numpy as jnp
from jax import lax
from jax.experimental import pallas as pl
from jax.experimental.pallas import tpu as pltpu
from jax.sharding import PartitionSpec as P

B = 2048
SUB = 64
TILE = 128
STRIP = 256
BATCH = 4
GROUP = 4
KEPT = {True: 24, False: 8}
EARLY = {True: 20, False: 4}
CELLS_X = 4
CELLS_Y = 8
CELLS = CELLS_X * CELLS_Y
FAR = 1.0e6

support_radius = 2.5
noise_level = 8.0
shift = noise_level + 1.0
profile_scale = 4.0 / support_radius**5
VMEM = pl.BlockSpec(memory_space=pltpu.VMEM)
SMEM = pl.BlockSpec(memory_space=pltpu.SMEM)
ANY = pl.BlockSpec(memory_space=pl.ANY)
LIMIT = 48 * 1024 * 1024


def from_behind(block, axis, distance):
    devices = range(lax.axis_size(axis))
    route = [(i - distance, i) for i in devices if i - distance in devices]
    return lax.ppermute(block, axis, route)


def exchange(values, mask, axis):
    devices = range(lax.axis_size(axis))
    return lax.ppermute(values, axis, [(i, i ^ mask) for i in devices])


def split3(values):
    high = values.astype(jnp.bfloat16)
    rest = values - high.astype(jnp.float32)
    middle = rest.astype(jnp.bfloat16)
    low = (rest - middle.astype(jnp.float32)).astype(jnp.bfloat16)
    return high, middle, low


def one_hot_strip(rank, start):
    place = lax.broadcasted_iota(jnp.int32, (TILE, B), 0).astype(jnp.bfloat16)
    one, zero = jnp.ones((), jnp.bfloat16), jnp.zeros((), jnp.bfloat16)
    blocks = []
    for t in range(STRIP // TILE):
        local = rank - (start + t * TILE)
        local = jnp.where((local >= 0) & (local < TILE), local, -1)
        local = local.astype(jnp.float32).astype(jnp.bfloat16)
        blocks.append(jnp.where(local == place, one, zero))
    return jnp.concatenate(blocks, axis=0)


def cell_of(values, cells):
    low = jnp.min(values, axis=1, keepdims=True)
    high = jnp.max(values, axis=1, keepdims=True)
    scaled = (values - low) * (cells / jnp.maximum(high - low, 1e-30))
    return jnp.minimum(jnp.floor(scaled), cells - 1.0)


def sort_kernel(
    count,
    active_ref,
    points_hbm,
    sides_ref,
    rows_ref,
    cols_ref,
    rank_ref,
    box_ref,
    vector_ref,
    feature_ref,
    split_ref,
    edge_ref,
    points_ref,
    arrived,
):
    column = lax.axis_index("blk")
    first = pl.multiple_of(lax.axis_index("rep") * 16, 16)
    locate = pltpu.make_async_copy(points_hbm, points_ref, arrived.at[0])
    locate.start()
    fetch = pltpu.make_async_copy(
        sides_ref.at[pl.ds(first, 16), :], vector_ref, arrived.at[1]
    )
    fetch.start()
    for own in (True, False):
        box_ref[2 if own else 3] = pair_flags(own, active_ref, column, count, box_ref.shape[1:])
    upper = lax.broadcasted_iota(jnp.int32, (TILE, TILE), 0) <= lax.broadcasted_iota(
        jnp.int32, (TILE, TILE), 1
    )
    upper = jnp.where(upper, 1.0, 0.0).astype(jnp.bfloat16)
    lower = lax.broadcasted_iota(jnp.int32, (CELLS, CELLS), 0) > lax.broadcasted_iota(
        jnp.int32, (CELLS, CELLS), 1
    )
    lower = jnp.where(lower, 1.0, 0.0).astype(jnp.bfloat16)
    number = lax.broadcasted_iota(jnp.int32, (CELLS, TILE), 0).astype(jnp.float32)
    feature_ref[16:32, :] = jnp.zeros((16, B), jnp.float32)
    split_ref[96:128, :] = jnp.zeros((32, B), jnp.bfloat16)
    locate.wait()
    for c in range(2):
        span = slice(c * B, (c + 1) * B)
        cell = cell_of(points_ref[0:1, span], CELLS_X) * CELLS_Y + cell_of(
            points_ref[1:2, span], CELLS_Y
        )
        base = jnp.zeros((CELLS, TILE), jnp.float32)
        chosen = [
            jnp.where(number == cell[:, t * TILE : (t + 1) * TILE], 1.0, 0.0)
            for t in range(B // TILE)
        ]
        counts = jnp.dot(
            jnp.concatenate(chosen, axis=0).astype(jnp.bfloat16),
            upper,
            preferred_element_type=jnp.float32,
        )
        place = []
        for t in range(B // TILE):
            count = counts[t * CELLS : (t + 1) * CELLS, :]
            place.append(count + base)
            base = base + count[:, TILE - 1 :]
        high = jnp.floor(base * (1.0 / 64.0))
        offset = jnp.dot(
            lower,
            jnp.concatenate([high, base - 64.0 * high], axis=1).astype(jnp.bfloat16),
            preferred_element_type=jnp.float32,
        )
        offset = 64.0 * offset[:, 0:TILE] + offset[:, TILE : 2 * TILE]
        for t in range(B // TILE):
            rank = jnp.sum(chosen[t] * (place[t] + (offset - 1.0)), axis=0, keepdims=True)
            rank_ref[0:1, c * B + t * TILE : c * B + (t + 1) * TILE] = rank.astype(jnp.int32)
        if c == 0:
            fetch.wait()
        feature_ref[0:16, :] = vector_ref[:, span]
        feature_ref[16:19, :] = points_ref[:, span]
        for k, part in enumerate(split3(feature_ref[...])):
            split_ref[32 * k : 32 * k + 32, :] = part
        rank = rank_ref[0:1, span]
        for k in range(B // STRIP):
            found = lax.dot_general(
                one_hot_strip(rank, k * STRIP),
                split_ref[...],
                (((1,), (1,)), ((), ())),
                preferred_element_type=jnp.float32,
            )
            found = found + pltpu.roll(found, 96, 1) + pltpu.roll(found, 64, 1)
            spot = slice(c * B + k * STRIP, c * B + (k + 1) * STRIP)
            cols_ref[spot, :] = found
            rows_ref[:, spot] = found.T[0:24, :]
            for t in range(STRIP // SUB):
                chunk = c * (B // SUB) + k * (STRIP // SUB) + t
                piece = found[t * SUB : (t + 1) * SUB, :]
                for e, edge in enumerate((jnp.min, jnp.max)):
                    value = edge(piece, axis=0, keepdims=True)
                    edge_ref[e, chunk : chunk + 1, :] = value
                    edge_ref[e, 64 + chunk : 65 + chunk, :] = value
            for t in range(STRIP // TILE):
                j = c * (B // TILE) + k * (STRIP // TILE) + t
                piece = found[t * TILE : (t + 1) * TILE, :]
                for e, edge in enumerate((jnp.min, jnp.max)):
                    box_ref[e, j : j + 1, :] = edge(piece, axis=0, keepdims=True)
    for e in range(2):
        turned = edge_ref[e].T
        for axis in range(3):
            rows_ref[19 + e : 20 + e, axis * TILE : (axis + 1) * TILE] = turned[
                16 + axis : 17 + axis, :
            ]


def sort_points(count, active, points, right_side):
    width = 2 * B
    return pl.pallas_call(
        partial(sort_kernel, count),
        out_shape=(
            jax.ShapeDtypeStruct((24, width), jnp.float32),
            jax.ShapeDtypeStruct((width, TILE), jnp.float32),
            jax.ShapeDtypeStruct((8, width), jnp.int32),
            jax.ShapeDtypeStruct((4, width // TILE, TILE), jnp.float32),
        ),
        in_specs=[SMEM, ANY, ANY],
        out_specs=(VMEM, VMEM, VMEM, VMEM),
        scratch_shapes=[
            pltpu.VMEM((16, width), jnp.float32),
            pltpu.VMEM((32, B), jnp.float32),
            pltpu.VMEM((128, B), jnp.bfloat16),
            pltpu.VMEM((2, TILE, TILE), jnp.float32),
            pltpu.VMEM((3, width), jnp.float32),
            pltpu.SemaphoreType.DMA((2,)),
        ],
        compiler_params=pltpu.CompilerParams(vmem_limit_bytes=LIMIT),
        name="sort_points",
    )(active, points, right_side)


def unsort_kernel(sorted_ref, rank_ref, out_ref, split_ref, total_ref):
    for c in range(2):
        span = slice(c * B, (c + 1) * B)
        for k, part in enumerate(split3(sorted_ref[:, span])):
            split_ref[16 * k : 16 * k + 16, :] = part
        rank = rank_ref[0:1, span]
        for k in range(B // STRIP):
            found = jnp.dot(
                split_ref[:, k * STRIP : (k + 1) * STRIP],
                one_hot_strip(rank, k * STRIP),
                preferred_element_type=jnp.float32,
            )
            total_ref[...] = found if k == 0 else total_ref[...] + found
        out_ref[:, span] = (total_ref[0:16, :] + total_ref[16:32, :]) + total_ref[32:48, :]


def unsort(values, rank):
    return pl.pallas_call(
        unsort_kernel,
        out_shape=jax.ShapeDtypeStruct(values.shape, jnp.float32),
        in_specs=[VMEM, VMEM],
        out_specs=VMEM,
        scratch_shapes=[pltpu.VMEM((48, B), jnp.bfloat16), pltpu.VMEM((48, B), jnp.float32)],
        compiler_params=pltpu.CompilerParams(vmem_limit_bytes=LIMIT),
        name="unsort",
    )(values, rank)


def pair_flags(own, active_ref, column, count, shape):
    is_second = lax.broadcasted_iota(jnp.int32, shape, 0) >= shape[0] // 2
    quarter = lax.broadcasted_iota(jnp.int32, shape, 1) // (TILE // 4)
    if own:
        flag = jnp.where(is_second == (quarter == 1), 1, active_ref[0, column])
        return jnp.where(quarter < 2, flag, 0).astype(jnp.float32)
    behind = jnp.maximum(column - 1, 0)
    has_behind = jnp.where(column >= 1, 1, 0)
    has_ahead = jnp.where(column + 1 < count, 1, 0)
    flag = jnp.zeros(shape, jnp.int32)
    for c in range(2):
        for q in range(4):
            if q < 2:
                value = active_ref[1 + 2 * q + c, behind] * has_behind
            else:
                value = active_ref[1 + 2 * c + (q - 2), column] * has_ahead
            flag = jnp.where((is_second == (c == 1)) & (quarter == q), value, flag)
    return flag.astype(jnp.float32)


def pair_table(own, box_ref, xyz_refs, null):
    shape = box_ref.shape[1:]
    lane = lax.broadcasted_iota(jnp.int32, shape, 1)
    total = jnp.zeros(shape, jnp.float32)
    for axis in range(3):
        low_t = box_ref[0, :, 16 + axis : 17 + axis]
        high_t = box_ref[1, :, 16 + axis : 17 + axis]
        span = slice(axis * TILE, (axis + 1) * TILE)
        edges = [[ref[19 + e : 20 + e, span] for e in range(2)] for ref in xyz_refs]
        if own:
            low_s, high_s = edges[0]
        else:
            is_before = lane[0:1] < SUB
            low_s, high_s = (jnp.where(is_before, edges[0][e], edges[1][e]) for e in range(2))
        gap = jnp.maximum(jnp.maximum(low_s - high_t, low_t - high_s), 0.0)
        total = total + gap * gap
    near = total <= support_radius * support_radius * (1.0 + 1e-4)
    near = near & (box_ref[2 if own else 3] > 0.0)
    upper = lax.broadcasted_iota(jnp.int32, (TILE, TILE), 0) <= lax.broadcasted_iota(
        jnp.int32, (TILE, TILE), 1
    )
    place = jnp.dot(
        jnp.where(near, 1.0, 0.0).astype(jnp.bfloat16),
        jnp.where(upper, 1.0, 0.0).astype(jnp.bfloat16),
        preferred_element_type=jnp.float32,
    ).astype(jnp.int32)
    value = jnp.where(near, lane, null)
    left = jnp.where(near, lane + 1 - place, 0)
    for bit in range(7):
        amount = 1 << bit
        next_value = pltpu.roll(value, TILE - amount, 1)
        next_left = pltpu.roll(left, TILE - amount, 1)
        arrives = (next_left & amount) > 0
        stays = (left & amount) == 0
        value = jnp.where(arrives, next_value, jnp.where(stays, value, null))
        left = jnp.where(arrives, next_left, jnp.where(stays, left, 0))
    return value + 256 * place[:, TILE - 1 :]


def apply_kernel(own, again, *refs):
    refs = list(refs)
    cols_ref, box_ref = refs[:2]
    del refs[:2]
    sources = 1 if own else 2
    xyz_refs = [refs.pop(0) for _ in range(sources)]
    vec_refs = [refs.pop(0) for _ in range(sources)]
    add_ref = None if own else refs.pop(0)
    sums = again and not own
    base_refs = [refs.pop(0) for _ in range(2)] if sums else None
    if again:
        list_ref, kept_ref = refs.pop(0), refs.pop(0)
    out_ref = refs.pop(0)
    if not again:
        table_ref, kept_ref = refs.pop(0), refs.pop(0)
    sums_ref = refs.pop(0) if sums else None
    left_xyz, right_xyz, left_w, right_w, target, bank, weights, total_ref, moved = refs[:9]
    rows = out_ref.shape[1] // TILE
    cells = rows // GROUP
    kept = KEPT[own]
    null = 2 * rows * sources
    lane = lax.broadcasted_iota(jnp.int32, (8, TILE), 1)
    is_left = lane < SUB

    def transfer(g):
        ends = (kept_ref.at[g], bank.at[g]) if again else (bank.at[g], kept_ref.at[g])
        return pltpu.make_async_copy(*ends, moved.at[g])

    if again:
        for g in range(EARLY[own]):
            transfer(g).start()
    else:
        list_ref, arrived = refs[9:]
        table_ref[...] = pair_table(own, box_ref, xyz_refs, null)
        load = pltpu.make_async_copy(table_ref, list_ref, arrived)
        load.start()

    def spread(values):
        turned = pltpu.roll(values, SUB, 1)
        mask = jnp.concatenate([is_left] * (values.shape[0] // 8), axis=0)
        zero = jnp.zeros_like(values)
        return (
            jnp.where(mask, values, zero),
            jnp.where(mask, zero, turned),
            jnp.where(mask, turned, zero),
            jnp.where(mask, zero, values),
        )

    def parts(values):
        high = values.astype(jnp.bfloat16)
        low = (values - high.astype(jnp.float32)).astype(jnp.bfloat16)
        return jnp.concatenate([high, low], axis=0)

    def prepare_xyz(s, spot, slot):
        xyz = spread(xyz_refs[s][16:24, spot])
        left_xyz[slot] = xyz[0]
        right_xyz[slot] = xyz[1]
        left_xyz[slot + 1] = xyz[2]
        right_xyz[slot + 1] = xyz[3]

    for s in range(sources):

        def prepare(g, carry):
            for u in range(4):
                t = g * 4 + u
                spot = pl.ds(pl.multiple_of(t * TILE, TILE), TILE)
                slot = 2 * (t + s * rows)
                if not again:
                    prepare_xyz(s, spot, slot)
                vec = spread(vec_refs[s][0:16, spot])
                left_w[slot] = parts(vec[0])
                right_w[slot] = parts(vec[1])
                left_w[slot + 1] = parts(vec[2])
                right_w[slot + 1] = parts(vec[3])
            return carry

        lax.fori_loop(0, rows // 4, prepare, 0)
    left_xyz[null] = jnp.where(is_left, FAR, 0.0)
    right_xyz[null] = jnp.where(is_left, 0.0, FAR)
    left_w[null] = jnp.zeros((32, TILE), jnp.bfloat16)
    right_w[null] = jnp.zeros((32, TILE), jnp.bfloat16)
    total_ref[...] = jnp.zeros_like(total_ref)
    bank[kept] = jnp.zeros(bank.shape[1:], jnp.bfloat16)
    weights[...] = jnp.zeros_like(weights)

    def members(cell):
        mirror = cell + 3 * cells // 2 - cells * (cell // (cells // 2))
        return cell, mirror, rows - 1 - mirror, rows - 1 - cell

    def batches(cell):
        count = list_ref[cell, 0]
        for j in members(cell)[1:]:
            count = jnp.maximum(count, list_ref[j, 0])
        return (count // 256 + BATCH - 1) // BATCH

    def aim(cell):
        for k, j in enumerate(members(cell)):
            spot = pl.ds(pl.multiple_of(j * TILE, TILE), TILE)
            for axis in range(3):
                target[3 * k + axis] = jnp.broadcast_to(
                    cols_ref[spot, 16 + axis : 17 + axis], (TILE, TILE)
                )

    def chunks(j, n, s):
        return list_ref[j, 4 * n + 2 * s] & 255, list_ref[j, 4 * n + 2 * s + 1] & 255

    def weigh(k, j, n):
        for s in range(2):
            first, second = chunks(j, n, s)
            weights[k, :, s * TILE : (s + 1) * TILE] = left_w[first] + right_w[second]

    def form(slot, k, j, n):
        for s in range(2):
            first, second = chunks(j, n, s)
            xyz = left_xyz[first] + right_xyz[second]
            here = slice(s * TILE, (s + 1) * TILE)
            for r in range(TILE // 16):
                span = slice(16 * r, 16 * r + 16)
                dx = target[3 * k, span, :] - xyz[0:1, :]
                dy = target[3 * k + 1, span, :] - xyz[1:2, :]
                dz = target[3 * k + 2, span, :] - xyz[2:3, :]
                square = jnp.maximum(dx * dx + dy * dy + dz * dz, 1e-30)
                distance = square * lax.rsqrt(square)
                inside = jnp.maximum(support_radius - distance, 0.0)
                inside = inside * inside
                value = (inside * inside) * (distance + 0.25 * support_radius)
                high = value.astype(jnp.bfloat16)
                low = (value - high.astype(jnp.float32)).astype(jnp.bfloat16)
                bank[slot, k, 16 * r : 16 * r + 16, here] = high
                bank[slot, k, TILE + 16 * r : TILE + 16 * r + 16, here] = low

    def apply(slot, k):
        both = lax.dot_general(
            weights[k],
            bank[slot, k],
            (((1,), (1,)), ((), ())),
            preferred_element_type=jnp.float32,
        )
        return both[:, 0:TILE] + both[:, TILE : 2 * TILE]

    def add(cell, images):
        for j, image in zip(members(cell), images):
            total_ref[j] += image

    if not again:
        load.wait()
    needed = lax.fori_loop(0, cells, lambda cell, n: n + batches(cell), 0)
    used = jnp.minimum(needed, kept)

    if again:
        early = EARLY[own]
        lax.fori_loop(early, used, lambda g, carry: (transfer(g).start(), carry)[1], 0)

        @pl.when(needed > kept)
        def _():
            for s in range(sources):

                def prepare_again(t, carry):
                    spot = pl.ds(pl.multiple_of(t * TILE, TILE), TILE)
                    prepare_xyz(s, spot, 2 * (t + s * rows))
                    return carry

                lax.fori_loop(0, rows, prepare_again, 0)

        def row_group(cell, g):
            def step(n, g):
                slot = jnp.minimum(g, kept)

                @pl.when(g < kept)
                def _():
                    transfer(g).wait()

                @pl.when(g >= kept)
                def _():
                    aim(cell)
                    for k, j in enumerate(members(cell)):
                        form(slot, k, j, n)

                for k, j in enumerate(members(cell)):
                    weigh(k, j, n)
                add(cell, [apply(slot, k) for k in range(GROUP)])
                return g + 1

            return lax.fori_loop(0, batches(cell), step, g)

        lax.fori_loop(0, cells, row_group, 0)
        lax.fori_loop(used, early, lambda g, carry: (transfer(g).wait(), carry)[1], 0)
    else:

        def row_group(cell, state):
            count = batches(cell)

            @pl.when(count > 0)
            def _():
                aim(cell)

            def step(n, state):
                g, last_slot, last_cell = state
                slot = jnp.minimum(g, kept)
                images = [apply(last_slot, k) for k in range(GROUP)]
                for k, j in enumerate(members(cell)):
                    weigh(k, j, n)
                    form(slot, k, j, n)
                add(last_cell, images)

                @pl.when(g < kept)
                def _():
                    transfer(g).start()

                return g + 1, slot, cell

            return lax.fori_loop(0, count, step, state)

        _, slot, cell = lax.fori_loop(0, cells, row_group, (0, kept, 0))
        add(cell, [apply(slot, k) for k in range(GROUP)])

    def finish(g, running):
        for u in range(4):
            j = g * 4 + u
            spot = pl.ds(pl.multiple_of(j * TILE, TILE), TILE)
            total = total_ref[j]
            image = (total[0:16, :] + total[16:32, :]) * profile_scale
            if own:
                held = (left_w[2 * j] + right_w[2 * j + 1]).astype(jnp.float32)
                image = image - (held[0:16, :] + held[16:32, :])
            else:
                image = image + add_ref[:, spot]
            out_ref[:, spot] = image
            if sums:
                side = base_refs[0][0:16, spot]
                first = base_refs[1][:, spot]
                running = (
                    running[0] + side * side,
                    running[1] + side * first,
                    running[2] + first * first,
                    running[3] + first * image,
                )
        return running

    zero = jnp.zeros((16, TILE), jnp.float32)
    result = lax.fori_loop(0, rows // 4, finish, (zero,) * 4 if sums else 0)
    if not again:
        lax.fori_loop(0, used, lambda g, carry: (transfer(g).wait(), carry)[1], 0)
    if sums:
        columns = lax.broadcasted_iota(jnp.int32, (16, TILE), 1)
        packed = zero
        for k in range(4):
            packed = jnp.where(columns == k, jnp.sum(result[k], axis=1, keepdims=True), packed)
        turned = jnp.concatenate([packed] + [zero] * 7, axis=0).T
        line = turned[0:1]
        for k in range(1, 4):
            line = line + pltpu.roll(turned[k : k + 1], 16 * k, 1)
        sums_ref[...] = jnp.broadcast_to(line, sums_ref.shape)


def apply_pairs(fixed, coords, vectors, added=None, bases=(), kept=None):
    own = added is None
    again = kept is not None
    operands = [*fixed, *coords, *vectors]
    operands += ([] if own else [added]) + list(bases)
    specs = [VMEM] * len(operands)
    rows = 2 * B // TILE
    slots = 2 * rows * len(coords) + 1
    out_shape = [jax.ShapeDtypeStruct((16, 2 * B), jnp.float32)]
    out_specs = [VMEM]
    bank = (GROUP, 2 * TILE, 2 * TILE)
    if again:
        operands += kept
        specs += [SMEM, ANY]
        scratch = []
    else:
        out_shape.append(jax.ShapeDtypeStruct((rows, TILE), jnp.int32))
        out_shape.append(jax.ShapeDtypeStruct((KEPT[own],) + bank, jnp.bfloat16))
        out_specs += [VMEM, ANY]
        scratch = [pltpu.SMEM((rows, TILE), jnp.int32), pltpu.SemaphoreType.DMA]
    if bases:
        out_shape.append(jax.ShapeDtypeStruct((256, TILE), jnp.float32))
        out_specs.append(VMEM)
    return pl.pallas_call(
        partial(apply_kernel, own, again),
        out_shape=out_shape,
        in_specs=specs,
        out_specs=out_specs,
        scratch_shapes=[
            pltpu.VMEM((slots, 8, TILE), jnp.float32),
            pltpu.VMEM((slots, 8, TILE), jnp.float32),
            pltpu.VMEM((slots, 32, TILE), jnp.bfloat16),
            pltpu.VMEM((slots, 32, TILE), jnp.bfloat16),
            pltpu.VMEM((3 * GROUP, TILE, TILE), jnp.float32),
            pltpu.VMEM((KEPT[own] + 1,) + bank, jnp.bfloat16),
            pltpu.VMEM((GROUP, 32, 2 * TILE), jnp.bfloat16),
            pltpu.VMEM((rows, 32, TILE), jnp.float32),
            pltpu.SemaphoreType.DMA((KEPT[own],)),
            *scratch,
        ],
        compiler_params=pltpu.CompilerParams(vmem_limit_bytes=LIMIT),
        name=("again_" if again else "apply_") + ("own" if own else "cross"),
    )(*operands)


def finish_kernel(lines_ref, sides_ref, *refs):
    posterior_ref, residual_ref, factor_ref = refs[8:]

    @pl.when(pl.program_id(0) == 0)
    def _():
        lines = lines_ref[...]
        row = lax.broadcasted_iota(jnp.int32, lines.shape, 0)
        sums = [
            jnp.sum(jnp.where((row & 3) == q, lines, 0.0), axis=0, keepdims=True)
            for q in range(4)
        ]
        sums = jnp.concatenate(sums + [jnp.zeros((4, lines.shape[1]), jnp.float32)], axis=0)
        sums = jnp.concatenate([sums, jnp.ones_like(sums)], axis=1)
        sums = jnp.concatenate([sums, jnp.ones((TILE - 8, TILE), jnp.float32)], axis=0).T
        s00, s01, s11, s12 = (sums[16 * k : 16 * k + 16] for k in range(4))
        image_norm = shift * s00 + s01
        alpha = s00 / image_norm
        keep = s01 / image_norm
        rr1 = alpha * alpha * (s11 - s01 * (s01 / s00))
        beta = rr1 / s00
        both = keep + beta
        curved = both * both * s01 - 2.0 * both * alpha * s11 + alpha * alpha * s12
        alpha1 = rr1 / (shift * rr1 * (1.0 + beta) + curved)
        factor_ref[0] = (s00 + s01) / image_norm - noise_level * alpha1 * both
        factor_ref[1] = noise_level * alpha1 * alpha
        factor_ref[2] = keep - shift * alpha1 * both
        factor_ref[3] = shift * alpha1 * alpha - alpha - alpha1 * both
        factor_ref[4] = alpha1 * alpha

    for member in range(4):

        @pl.when(lax.axis_index("rep") == member)
        def _():
            for q in range(4):
                rows = slice(16 * q, 16 * q + 16)
                factor = [factor_ref[k, :, q : q + 1] for k in range(5)]
                side = sides_ref[rows, :]
                first = refs[q ^ member][...]
                second = refs[4 + (q ^ member)][...]
                posterior_ref[rows, :] = factor[0] * side + factor[1] * first
                residual_ref[rows, :] = (
                    factor[2] * side + factor[3] * first + factor[4] * second
                )


def finish_sides(lines, right_side, pieces):
    width = 1024
    full = pl.BlockSpec((64, width), lambda i: (0, i))
    part = pl.BlockSpec((16, width), lambda i: (0, i))
    shape = jax.ShapeDtypeStruct(right_side.shape, jnp.float32)
    return pl.pallas_call(
        finish_kernel,
        grid=(right_side.shape[1] // width,),
        out_shape=(shape, shape),
        in_specs=[pl.BlockSpec(lines.shape, lambda i: (0, 0)), full] + [part] * 8,
        out_specs=(full, full),
        scratch_shapes=[pltpu.VMEM((5, 16, TILE), jnp.float32)],
        compiler_params=pltpu.CompilerParams(vmem_limit_bytes=LIMIT),
        name="finish_sides",
    )(lines, right_side, *pieces)


def shards(right_side, points, active):
    def spread(values):
        return [values] + [exchange(values, mask, "rep") for mask in (1, 2, 3)]

    def neighbours(values):
        return from_behind(values, "blk", 1), from_behind(values, "blk", -1)

    rows, cols, rank, box = sort_points(lax.axis_size("blk"), active.T, points, right_side)
    around = neighbours(rows)
    fixed = (cols, box)
    part, *kept_own = apply_pairs(fixed, (rows,), (rows,))
    w0, *kept_cross = apply_pairs(fixed, around, around, part)
    w0_around = neighbours(w0)
    w0_pieces = spread(unsort(w0, rank))
    (part,) = apply_pairs(fixed, (rows,), (w0,), kept=kept_own)
    w1, line = apply_pairs(fixed, around, w0_around, part, (rows, w0), kept_cross)
    mine = unsort(w1, rank)
    w1_pieces = spread(mine)
    lines = lax.all_to_all(line[:, 0:64], ("blk", "rep"), 0, 0, tiled=True)
    return finish_sides(lines, right_side, w0_pieces + w1_pieces)


def solution(mesh):
    return jax.shard_map(
        shards,
        mesh=mesh,
        in_specs=(P(None, "blk"), P(None, "blk"), P()),
        out_specs=(P(None, "blk"), P(None, "blk")),
        check_vma=False,
    )
```
